32 devices in a mesh: occ: 8 (over z, y), aux: 4 (over x, core).
Axes of the slice: x: 2, y: 2, z: 4, core: 2. Of those that a mesh axis runs over, the one named last changes fastest.
Arguments:
- orbital_b: bfloat16 [64, 3072, 768], P('occ', 'aux'), may hold values from -0.75 to 0.75
- occ_energy: float32 [64], replicated, may hold values from -3 to -0.5
- vir_energy: float32 [768], replicated, may hold values from 0.2 to 3
Outputs:
- gradient_term: bfloat16 [64, 3072, 768], P('occ', 'aux')
The draws below stay inside these ranges and needn't reach their ends.
All inputs are finite; a program needn't handle non-finite values.
Results may differ from the reference program's by a relative error of at most 0.0044.
Values may be sent and summed in bfloat16 or wider, within the bound.
No kernel may reach another device: no remote copies, remote signals or barrier semaphores. Data moves between devices by JAX's collectives and lax.ppermute only.
A program may use at most 128 MiB of HBM per device.

```python
import jax
import jax.numpy as jnp
from jax import lax

I_DEV = 8
VIR = 768
NAUX = 3072
OCC = 64
N_OCC = 8


def level_of(key, dims, pieces, least, largest):
    def one(axis_at, parts):
        steps = jax.random.uniform(jax.random.fold_in(jax.random.fold_in(key, 6), axis_at), (parts,), jnp.float32, least / len(pieces), largest / len(pieces))
        return jnp.repeat(jnp.exp(steps), dims[axis_at] // parts).reshape((-1,) + (1,) * (len(dims) - axis_at - 1))

    loudness = one(*pieces[0])
    for cut in pieces[1:]:
        loudness = loudness * one(*cut)
    return loudness


def scatter_about(rng, dims, deviation, bound, shards=(), dtype=jnp.bfloat16):
    values = deviation * jax.random.normal(rng, dims, jnp.float32)
    if shards:
        values = values * level_of(rng, dims, shards, -0.22, 0.18)
    return jnp.clip(values, -bound, bound).astype(dtype)


def setup_inputs(seed: int = 0) -> dict:
    splits = jax.random.split(jax.random.key(seed), 4)
    return {
        "orbital_b": scatter_about(splits[0], (OCC, NAUX, VIR), (NAUX ** -0.25), 0.75, ((0, 8), (1, 4))),
        "occ_energy": jnp.clip(jax.random.uniform(splits[1], (OCC,), jnp.float32, -3.0, -0.5), -3.0, -0.5),
        "vir_energy": jnp.clip(jax.random.uniform(splits[2], (VIR,), jnp.float32, 0.2, 3.0), 0.2, 3.0),
    }


def reference(orbital_b, occ_energy, vir_energy):
    leaders = orbital_b[::I_DEV]
    zero_block = jnp.zeros_like(leaders[:1])
    before = jnp.concatenate([zero_block, leaders[:-1]], axis=0)
    follow = jnp.concatenate([leaders[1:], zero_block], axis=0)
    partner_b = jnp.stack([before, follow], axis=1)
    leader_energy = occ_energy[::I_DEV]
    energy_before = jnp.concatenate([leader_energy[:1], leader_energy[:-1]])
    energy_follow = jnp.concatenate([leader_energy[1:], leader_energy[-1:]])
    partner_energy = jnp.stack([energy_before, energy_follow], axis=1)
    blocks = orbital_b.reshape(N_OCC, I_DEV, NAUX, VIR)
    block_energy = occ_energy.reshape(N_OCC, I_DEV)

    def per_block(packed):
        block, energy, partners, pair_energy = packed
        block_wide = block.astype(jnp.float32)
        partner_wide = partners.astype(jnp.float32)
        integral = jnp.einsum("iPa,pPb->iapb", block_wide, partner_wide, precision=lax.Precision.HIGHEST)
        denominator = (vir_energy[None, :, None, None] + vir_energy[None, None, None, :]
                       - energy[:, None, None, None] - pair_energy[None, None, :, None])
        amplitude = (integral / denominator).astype(jnp.bfloat16)
        result = jnp.einsum("iapb,pPb->iPa", amplitude.astype(jnp.float32), partner_wide, precision=lax.Precision.HIGHEST)
        return result.astype(jnp.bfloat16)

    output = lax.map(per_block, (blocks, block_energy, partner_b, partner_energy))
    return output.reshape(N_OCC * I_DEV, NAUX, VIR)
```

```python
import functools

import jax
import jax.numpy as jnp
from jax import lax
from jax.experimental import pallas as pl
from jax.experimental.pallas import tpu as pltpu
from jax.sharding import PartitionSpec as P

VMEM_BYTES = 48 * 1024 * 1024


def shifted(value, axis, steps):
    count = lax.axis_size(axis)
    initial, last = (max(0, -steps), min(count, count - steps))
    return lax.ppermute(value, axis, [(source, source + steps) for source in range(initial, last)])


def tile_of(width):
    return next(tile for tile in (256, 128, width) if width % tile == 0)


def partial_kernel(place, near, far, near_b, far_b, after, exact, rounded):
    total = jnp.dot(near[...], near_b[0], preferred_element_type=jnp.float32)
    total += jnp.dot(far[...], far_b[0], preferred_element_type=jnp.float32)
    exact[0] = total
    rounded[0] = total.astype(jnp.bfloat16)


def partial_integrals(place, near, far, orbital_b, fetched, first, count, after):
    width, depth = near.shape
    virs = orbital_b.shape[2]
    tile = tile_of(virs)
    grid_spec = pltpu.PrefetchScalarGridSpec(
        num_scalar_prefetch=1,
        grid=(count, virs // tile),
        in_specs=[
            pl.BlockSpec((width, depth), lambda i, t, place: (0, 0)),
            pl.BlockSpec((width, depth), lambda i, t, place: (0, 0)),
            pl.BlockSpec((1, depth, tile), lambda i, t, place: (place[0] + first + i, 0, t)),
            pl.BlockSpec((1, depth, tile), lambda i, t, place: (first + i, 0, t)),
            pl.BlockSpec(memory_space=pl.ANY),
        ],
        out_specs=[pl.BlockSpec((1, width, tile), lambda i, t, place: (i, 0, t))] * 2,
    )
    flops = 4 * count * width * depth * virs
    return pl.pallas_call(
        partial_kernel,
        grid_spec=grid_spec,
        out_shape=[
            jax.ShapeDtypeStruct((count, width, virs), jnp.float32),
            jax.ShapeDtypeStruct((count, width, virs), jnp.bfloat16),
        ],
        compiler_params=pltpu.CompilerParams(vmem_limit_bytes=VMEM_BYTES),
        cost_estimate=pl.CostEstimate(flops=flops, bytes_accessed=flops // depth * 4, transcendentals=0),
    )(place, near, far, orbital_b, fetched, after)


def gamma_kernel(pieces, orbital, virs, place, energies, row, column, leaders, *refs):
    sums, out, amplitude = refs[: 2 * len(pieces)], refs[-2], refs[-1]
    own_energy = energies[place[1] + orbital]
    for at, (partner, start, stop) in enumerate(pieces):
        exact, received = sums[2 * at], sums[2 * at + 1]
        denominator = (row[...] + column[start:stop]) - own_energy - energies[place[2 + partner]]
        integral = exact[0] + received[0].astype(jnp.float32)
        amplitude[partner * virs + start : partner * virs + stop] = (integral / denominator).astype(jnp.bfloat16)
    total = jnp.dot(leaders[...], amplitude[...], preferred_element_type=jnp.float32).astype(jnp.bfloat16)
    depth = out.shape[1]
    out[0] = total[:depth]
    out[1] = total[depth:]


def gamma_rows(place, energies, row, column, leaders, pieces, orbital, sums):
    depth, width = leaders.shape[0] // 2, leaders.shape[1]
    virs = width // 2
    tile = tile_of(virs)
    in_specs = [
        pl.BlockSpec(memory_space=pltpu.SMEM),
        pl.BlockSpec((1, tile), lambda t, place: (0, t)),
        pl.BlockSpec((virs, 1), lambda t, place: (0, 0)),
        pl.BlockSpec(leaders.shape, lambda t, place: (0, 0)),
    ]
    operands = []
    for (partner, start, stop), (exact, received, at) in zip(pieces, sums):
        spec = pl.BlockSpec((1, stop - start, tile), functools.partial(lambda at, t, place: (at, 0, t), at))
        in_specs += [spec, spec]
        operands += [exact, received]
    flops = 4 * depth * width * virs
    return pl.pallas_call(
        functools.partial(gamma_kernel, pieces, orbital, virs),
        grid_spec=pltpu.PrefetchScalarGridSpec(
            num_scalar_prefetch=1,
            grid=(virs // tile,),
            in_specs=in_specs,
            out_specs=pl.BlockSpec((2, depth, tile), lambda t, place: (0, 0, t)),
            scratch_shapes=[pltpu.VMEM((width, tile), jnp.bfloat16)],
        ),
        out_shape=jax.ShapeDtypeStruct((2, depth, virs), jnp.bfloat16),
        compiler_params=pltpu.CompilerParams(vmem_limit_bytes=VMEM_BYTES),
        cost_estimate=pl.CostEstimate(flops=flops, bytes_accessed=12 * width * virs, transcendentals=0),
    )(place, energies, row, column, leaders, *operands)


def shards(orbital_b, occ_energy, vir_energy):
    occ_index = lax.axis_index("occ")
    aux_index = lax.axis_index("aux")
    occ_count = lax.axis_size("occ")
    aux_count = lax.axis_size("aux")
    chips = aux_count // 2
    rows, depth, virs = orbital_b.shape
    half = rows // 2
    core = aux_index % 2

    def to_mate(value):
        return lax.ppermute(value, "aux", [(at, at ^ 1) for at in range(aux_count)])

    def to_chip(value, steps):
        return lax.ppermute(value, "aux", [(at, (at + 2 * steps) % aux_count) for at in range(aux_count)])

    place = jnp.stack([
        core * half,
        occ_index * rows + core * half,
        jnp.maximum(occ_index - 1, 0) * rows,
        jnp.minimum(occ_index + 1, occ_count - 1) * rows,
    ]).astype(jnp.int32)

    cut = virs // 3 if virs % 384 == 0 else virs // 2
    pieces = [(0, 0, cut), (0, cut, virs), (1, 0, virs)]
    leading = orbital_b[0].T
    near = [shifted(leading[start:stop], "occ", 1 - 2 * partner) for partner, start, stop in pieces]
    far = [to_mate(value) for value in near]
    given = lax.dynamic_slice_in_dim(orbital_b, (1 - core) * half, half)
    fetched = to_mate(given)

    steps = [(0, 0, 1), (0, 1, half - 1)]
    steps += [(piece, at, 1) for piece in (1, 2) for at in range(half)]
    arrived = []
    found = {}
    for at, (piece, first, count) in enumerate(steps):
        after = arrived[at - 2] if at >= 2 else vir_energy
        exact, rounded = partial_integrals(place, near[piece], far[piece], orbital_b, fetched, first, count, after)
        for step in range(1, chips - 1):
            exact = exact + to_chip(rounded, step).astype(jnp.float32)
        received = to_chip(rounded, chips - 1) if chips > 1 else jnp.zeros_like(rounded)
        arrived.append(received)
        for offset in range(count):
            found[piece, first + offset] = (exact, received, offset)

    leaders = jnp.concatenate([jnp.concatenate(near, axis=0), jnp.concatenate(far, axis=0)], axis=1).T
    row, column = vir_energy[None, :], vir_energy[:, None]
    out = jnp.zeros_like(orbital_b)
    for orbital in range(half):
        sums = [found[piece, orbital] for piece in range(len(pieces))]
        both = gamma_rows(place, occ_energy, row, column, leaders, pieces, orbital, sums)
        out = lax.dynamic_update_slice_in_dim(out, both[:1], core * half + orbital, 0)
        out = lax.dynamic_update_slice_in_dim(out, to_mate(both[1:]), (1 - core) * half + orbital, 0)
    return out


def solution(mesh):
    placed = (P("occ", "aux", None), P(), P())
    return jax.shard_map(
        shards, mesh=mesh, in_specs=placed, out_specs=P("occ", "aux", None), check_vma=False
    )
```

```python
import functools

import jax
import jax.numpy as jnp
from jax import lax
from jax.experimental import pallas as pl
from jax.experimental.pallas import tpu as pltpu
from jax.sharding import PartitionSpec as P

VMEM_BYTES = 56 * 1024 * 1024

OWN, MATE, OWN_ENERGY, PARTNER_ENERGY = 0, 1, 2, 3


def shifted(value, axis, steps):
    count = lax.axis_size(axis)
    initial, last = (max(0, -steps), min(count, count - steps))
    return lax.ppermute(value, axis, [(source, source + steps) for source in range(initial, last)])


def params():
    return pltpu.CompilerParams(vmem_limit_bytes=VMEM_BYTES)


def take_kernel(place, source, after, out):
    out[...] = source[...].reshape(out.shape)


def leader_columns(place, orbital_b, start, stop, after):
    depth = orbital_b.shape[1]
    width = 128 if (start % 128 == 0 and stop % 128 == 0) else stop - start
    return pl.pallas_call(
        take_kernel,
        grid_spec=pltpu.PrefetchScalarGridSpec(
            num_scalar_prefetch=1,
            grid=((stop - start) // width,),
            in_specs=[
                pl.BlockSpec((1, depth, width), lambda t, place: (0, 0, start // width + t)),
                pl.BlockSpec(memory_space=pl.ANY),
            ],
            out_specs=pl.BlockSpec((depth, width), lambda t, place: (0, t)),
        ),
        out_shape=jax.ShapeDtypeStruct((depth, stop - start), orbital_b.dtype),
        compiler_params=params(),
        cost_estimate=pl.CostEstimate(flops=0, bytes_accessed=4 * depth * (stop - start), transcendentals=0),
    )(place, orbital_b, after)


def mate_orbitals(place, orbital_b, first, count, after):
    depth, virs = orbital_b.shape[1:]
    return pl.pallas_call(
        take_kernel,
        grid_spec=pltpu.PrefetchScalarGridSpec(
            num_scalar_prefetch=1,
            grid=(count,),
            in_specs=[
                pl.BlockSpec((1, depth, virs), lambda i, place: (place[MATE] + first + i, 0, 0)),
                pl.BlockSpec(memory_space=pl.ANY),
            ],
            out_specs=pl.BlockSpec((1, depth, virs), lambda i, place: (i, 0, 0)),
        ),
        out_shape=jax.ShapeDtypeStruct((count, depth, virs), orbital_b.dtype),
        compiler_params=params(),
        cost_estimate=pl.CostEstimate(flops=0, bytes_accessed=4 * count * depth * virs, transcendentals=0),
    )(place, orbital_b, after)


def partial_kernel(place, near, far, near_b, far_b, after, before, exact, rounded):
    total = jnp.dot(near[...], near_b[0], preferred_element_type=jnp.float32)
    total += jnp.dot(far[...], far_b[0], preferred_element_type=jnp.float32)
    exact[0] = total
    rounded[0] = total.astype(jnp.bfloat16)


def partial_integrals(place, near, far, orbital_b, fetched, first, count, offset, start, stop, after, before):
    width, depth = stop - start, near.shape[1]
    virs = orbital_b.shape[2]
    tile = virs if count > 1 else virs // 2 if virs % 256 == 0 else virs
    grid_spec = pltpu.PrefetchScalarGridSpec(
        num_scalar_prefetch=1,
        grid=(count, virs // tile),
        in_specs=[
            pl.BlockSpec((width, depth), lambda i, t, place: (start // width, 0)),
            pl.BlockSpec((width, depth), lambda i, t, place: (start // width, 0)),
            pl.BlockSpec((1, depth, tile), lambda i, t, place: (place[OWN] + first + i, 0, t)),
            pl.BlockSpec((1, depth, tile), lambda i, t, place: (offset + i, 0, t)),
            pl.BlockSpec(memory_space=pl.ANY),
            pl.BlockSpec(memory_space=pl.ANY),
        ],
        out_specs=[pl.BlockSpec((1, width, tile), lambda i, t, place: (i, 0, t))] * 2,
    )
    return pl.pallas_call(
        partial_kernel,
        grid_spec=grid_spec,
        out_shape=[
            jax.ShapeDtypeStruct((count, width, virs), jnp.float32),
            jax.ShapeDtypeStruct((count, width, virs), jnp.bfloat16),
        ],
        compiler_params=params(),
        cost_estimate=pl.CostEstimate(
            flops=4 * count * width * depth * virs,
            bytes_accessed=count * virs * (4 * depth + 6 * width),
            transcendentals=0,
        ),
    )(place, near, far, orbital_b, fetched, after, before)


def gamma_kernel(spans, orbital, halves, has_base, place, energies, row, column, *refs):
    refs = list(refs)
    leaders = [refs.pop(0) for _ in range(halves)]
    bases = [refs.pop(0) for _ in range(halves)] if has_base else None
    sums = [(refs.pop(0), refs.pop(0)) for _ in spans]
    amplitude = refs.pop()
    outs = refs[-halves:]
    own_energy = energies[place[OWN_ENERGY] + orbital]
    at = 0
    for (partner, start, stop), (exact, received) in zip(spans, sums):
        denominator = (row[...] + column[start:stop]) - own_energy - energies[place[PARTNER_ENERGY + partner]]
        integral = exact[0] + received[0].astype(jnp.float32)
        amplitude[at : at + stop - start] = (integral / denominator).astype(jnp.bfloat16)
        at += stop - start
    for half in range(halves):
        total = jnp.dot(leaders[half][...], amplitude[...], preferred_element_type=jnp.float32)
        if has_base:
            total += bases[half][...]
        outs[half][...] = total.astype(outs[half].dtype).reshape(outs[half].shape)


def gamma_rows(place, energies, row, column, leaders, at, spans, orbital, sums, bases=None, out_types=None, whole=None, previous=None):
    depth = leaders[0].shape[0]
    virs = row.shape[1]
    width = sum(stop - start for _, start, stop in spans)
    tile = next(tile for tile in (256, 128, virs) if virs % tile == 0)
    flat = pl.BlockSpec((depth, tile), lambda t, place: (0, t))
    in_specs = [
        pl.BlockSpec(memory_space=pltpu.SMEM),
        pl.BlockSpec((1, tile), lambda t, place: (0, t)),
        pl.BlockSpec((virs, 1), lambda t, place: (0, 0)),
    ]
    in_specs += [pl.BlockSpec((depth, width), lambda t, place: (0, at // width))] * len(leaders)
    operands = list(leaders)
    if bases is not None:
        in_specs += [flat] * len(bases)
        operands += bases
    for (_, start, stop), (exact, received, offset) in zip(spans, sums):
        spec = pl.BlockSpec((1, stop - start, tile), functools.partial(lambda offset, t, place: (offset, 0, t), offset))
        in_specs += [spec, spec]
        operands += [exact, received]
    out_shape = [jax.ShapeDtypeStruct((depth, virs), kind) for kind in out_types]
    out_specs = [flat] * len(leaders)
    aliases = {}
    if whole is not None:
        out_shape[0] = jax.ShapeDtypeStruct(whole, out_types[0])
        out_specs[0] = pl.BlockSpec((1, depth, tile), lambda t, place: (place[OWN] + orbital, 0, t))
        if previous is not None:
            in_specs.append(pl.BlockSpec(memory_space=pl.ANY))
            operands.append(previous)
            aliases = {4 + len(operands) - 1: 0}
    return pl.pallas_call(
        functools.partial(gamma_kernel, spans, orbital, len(leaders), bases is not None),
        grid_spec=pltpu.PrefetchScalarGridSpec(
            num_scalar_prefetch=1,
            grid=(virs // tile,),
            in_specs=in_specs,
            out_specs=out_specs,
            scratch_shapes=[pltpu.VMEM((width, tile), jnp.bfloat16)],
        ),
        out_shape=out_shape,
        input_output_aliases=aliases,
        compiler_params=params(),
        cost_estimate=pl.CostEstimate(
            flops=2 * len(leaders) * depth * width * virs,
            bytes_accessed=6 * width * virs + 4 * len(leaders) * depth * virs,
            transcendentals=0,
        ),
    )(place, energies, row, column, *operands)


def shards(orbital_b, occ_energy, vir_energy):
    occ_index = lax.axis_index("occ")
    aux_index = lax.axis_index("aux")
    occ_count = lax.axis_size("occ")
    aux_count = lax.axis_size("aux")
    chips = aux_count // 2
    rows, depth, virs = orbital_b.shape
    half = rows // 2
    core = aux_index % 2

    def to_mate(value):
        return lax.ppermute(value, "aux", [(at, at ^ 1) for at in range(aux_count)])

    def to_chip(value):
        return lax.ppermute(value, "aux", [(at, (at + 2) % aux_count) for at in range(aux_count)])

    place = jnp.stack([
        core * half,
        (1 - core) * half,
        occ_index * rows + core * half,
        jnp.maximum(occ_index - 1, 0) * rows,
        jnp.minimum(occ_index + 1, occ_count - 1) * rows,
    ]).astype(jnp.int32)

    unit = virs // 6 if virs % 768 == 0 else virs // 3
    cuts = (0, unit, 3 * unit, virs) if 3 * unit < virs else (0, unit, virs)
    spans = [(0, start, stop) for start, stop in zip(cuts, cuts[1:])] + [(1, 0, virs)]
    final = virs - virs // 3
    groups = [(0, half // 2), (half // 2, half - half // 2)]

    near, far, fetched = [], [], []

    def bring(after):
        partner, start, stop = spans[len(near)]
        columns = leader_columns(place, orbital_b, start, stop, after)
        near.append(shifted(columns, "occ", 1 - 2 * partner))
        far.append(to_mate(near[-1]))
        return columns

    columns = bring(vir_energy)
    for first, count in groups:
        fetched.append(to_mate(mate_orbitals(place, orbital_b, first, count, columns)))

    steps = [(piece, 0, spans[piece][2] - spans[piece][1], *group) for piece in range(len(spans) - 1) for group in groups]
    steps += [(len(spans) - 1, 0, virs, at, 1) for at in range(half - 1)]
    steps += [(len(spans) - 1, 0, final, half - 1, 1), (len(spans) - 1, final, virs, half - 1, 1)]
    ahead = 2 if chips == 2 else 1
    arrived = []
    found = {}
    rounded = vir_energy
    for at, (piece, start, stop, first, count) in enumerate(steps):
        after = arrived[at - ahead] if at >= ahead else vir_energy
        group = max(at for at, (lowest, _) in enumerate(groups) if lowest <= first)
        exact, rounded = partial_integrals(
            place, near[piece].T, far[piece].T, orbital_b, fetched[group],
            first, count, first - groups[group][0], start, stop, after, rounded,
        )
        if len(near) < len(spans) and first == 0:
            bring(rounded)
        received = to_chip(rounded) if chips > 1 else jnp.zeros_like(rounded)
        for _ in range(chips - 2):
            exact = exact + received.astype(jnp.float32)
            received = to_chip(received)
        arrived.append(received if chips <= 2 else exact)
        for offset in range(count):
            partner, lowest, _ = spans[piece]
            found.setdefault(first + offset, []).append(((partner, lowest + start, lowest + stop), (exact, received, offset)))

    near_all, far_all = jnp.concatenate(near, axis=1), jnp.concatenate(far, axis=1)
    fixed = (place, occ_energy, vir_energy[None, :], vir_energy[:, None])
    narrow = orbital_b.dtype
    out, returned = None, []
    for orbital in range(half):
        parts, sums = zip(*found[orbital])
        if orbital < half - 1:
            out, other = gamma_rows(
                *fixed, [near_all, far_all], 0, parts, orbital, sums,
                out_types=[narrow] * 2, whole=orbital_b.shape, previous=out,
            )
        else:
            lacks = virs - final
            bases = gamma_rows(
                *fixed, [near_all[:, :-lacks], far_all[:, :-lacks]], 0, parts[:-1], orbital, sums[:-1],
                out_types=[jnp.float32] * 2,
            )
            tail = (2 * virs - lacks, parts[-1:], orbital, sums[-1:])
            (other,) = gamma_rows(*fixed, [far_all], *tail, bases=bases[1:], out_types=[narrow])
            (out,) = gamma_rows(
                *fixed, [near_all], *tail, bases=bases[:1], out_types=[narrow], whole=orbital_b.shape, previous=out
            )
        returned.append(to_mate(other))
        if orbital > 0:
            out = lax.dynamic_update_slice_in_dim(out, returned[orbital - 1][None], (1 - core) * half + orbital - 1, 0)
    return lax.dynamic_update_slice_in_dim(out, returned[-1][None], (1 - core) * half + half - 1, 0)


def solution(mesh):
    placed = (P("occ", "aux", None), P(), P())
    return jax.shard_map(
        shards, mesh=mesh, in_specs=placed, out_specs=P("occ", "aux", None), check_vma=False
    )
```

```python
import functools

import jax
import jax.numpy as jnp
from jax import lax
from jax.experimental import pallas as pl
from jax.experimental.pallas import tpu as pltpu
from jax.sharding import PartitionSpec as P

VMEM_BYTES = 56 * 1024 * 1024

BRIEF = pl.CostEstimate(flops=0, bytes_accessed=0, transcendentals=0)

OWN, MATE, OWN_ENERGY, PARTNER_ENERGY = 0, 1, 2, 3


def shifted(value, axis, steps):
    count = lax.axis_size(axis)
    initial, last = (max(0, -steps), min(count, count - steps))
    return lax.ppermute(value, axis, [(source, source + steps) for source in range(initial, last)])


def params():
    return pltpu.CompilerParams(vmem_limit_bytes=VMEM_BYTES)


def take_kernel(place, source, after, out):
    out[...] = source[...].reshape(out.shape)


def columns_kernel(source, after, out):
    out[...] = source[0]


def leader_columns(orbital_b, start, stop, after):
    depth = orbital_b.shape[1]
    width = 128 if (start % 128 == 0 and stop % 128 == 0) else stop - start
    return pl.pallas_call(
        columns_kernel,
        grid=((stop - start) // width,),
        in_specs=[
            pl.BlockSpec((1, depth, width), lambda t: (0, 0, start // width + t)),
            pl.BlockSpec(memory_space=pl.ANY),
        ],
        out_specs=pl.BlockSpec((depth, width), lambda t: (0, t)),
        out_shape=jax.ShapeDtypeStruct((depth, stop - start), orbital_b.dtype),
        compiler_params=params(),
        cost_estimate=BRIEF,
    )(orbital_b, after)


def mate_orbitals(place, orbital_b, first, count, after):
    depth, virs = orbital_b.shape[1:]
    return pl.pallas_call(
        take_kernel,
        grid_spec=pltpu.PrefetchScalarGridSpec(
            num_scalar_prefetch=1,
            grid=(count,),
            in_specs=[
                pl.BlockSpec((1, depth, virs), lambda i, place: (place[MATE] + first + i, 0, 0)),
                pl.BlockSpec(memory_space=pl.ANY),
            ],
            out_specs=pl.BlockSpec((1, depth, virs), lambda i, place: (i, 0, 0)),
        ),
        out_shape=jax.ShapeDtypeStruct((count, depth, virs), orbital_b.dtype),
        compiler_params=params(),
        cost_estimate=pl.CostEstimate(flops=0, bytes_accessed=4 * count * depth * virs, transcendentals=0),
    )(place, orbital_b, after)


def partial_kernel(place, near, far, near_b, far_b, *refs):
    exact, rounded = refs[-2:]
    total = jnp.dot(near[...], near_b[0], preferred_element_type=jnp.float32)
    total += jnp.dot(far[...], far_b[0], preferred_element_type=jnp.float32)
    exact[0] = total
    rounded[0] = total.astype(jnp.bfloat16)


def partial_integrals(place, near, far, orbital_b, fetched, first, count, offset, after):
    width, depth = near.shape
    virs = orbital_b.shape[2]
    tile = virs if count > 1 or width < virs else virs // 2 if virs % 256 == 0 else virs
    grid_spec = pltpu.PrefetchScalarGridSpec(
        num_scalar_prefetch=1,
        grid=(count, virs // tile),
        in_specs=[
            pl.BlockSpec((width, depth), lambda i, t, place: (0, 0)),
            pl.BlockSpec((width, depth), lambda i, t, place: (0, 0)),
            pl.BlockSpec((1, depth, tile), lambda i, t, place: (place[OWN] + first + i, 0, t)),
            pl.BlockSpec((1, depth, tile), lambda i, t, place: (offset + i, 0, t)),
        ] + [pl.BlockSpec(memory_space=pl.ANY)] * len(after),
        out_specs=[pl.BlockSpec((1, width, tile), lambda i, t, place: (i, 0, t))] * 2,
    )
    return pl.pallas_call(
        partial_kernel,
        grid_spec=grid_spec,
        out_shape=[
            jax.ShapeDtypeStruct((count, width, virs), jnp.float32),
            jax.ShapeDtypeStruct((count, width, virs), jnp.bfloat16),
        ],
        compiler_params=params(),
        cost_estimate=BRIEF,
    )(place, near, far, orbital_b, fetched, *after)


def gamma_kernel(spans, orbital, halves, has_base, place, energies, row, column, *refs):
    refs = list(refs)
    leaders = [refs.pop(0) for _ in range(halves)]
    bases = [refs.pop(0) for _ in range(halves)] if has_base else None
    sums = [(refs.pop(0), refs.pop(0)) for _ in spans]
    amplitude = refs.pop()
    outs = refs[-halves:]
    own_energy = energies[place[OWN_ENERGY] + orbital]
    at = 0
    for (partner, start, stop), (exact, received) in zip(spans, sums):
        denominator = (row[...] + column[start:stop]) - own_energy - energies[place[PARTNER_ENERGY + partner]]
        integral = exact[0] + received[0].astype(jnp.float32)
        amplitude[at : at + stop - start] = (integral / denominator).astype(jnp.bfloat16)
        at += stop - start
    for half in range(halves):
        total = jnp.dot(leaders[half][...], amplitude[...], preferred_element_type=jnp.float32)
        if has_base:
            total += bases[half][...]
        outs[half][...] = total.astype(outs[half].dtype).reshape(outs[half].shape)


def gamma_rows(place, energies, row, column, leaders, spans, orbital, sums, bases=None, out_types=None, whole=None, previous=None, tile=None):
    depth = leaders[0].shape[0]
    virs = row.shape[1]
    width = sum(stop - start for _, start, stop in spans)
    tile = tile or next(tile for tile in (256, 128, virs) if virs % tile == 0)
    flat = pl.BlockSpec((depth, tile), lambda t, place: (0, t))
    in_specs = [
        pl.BlockSpec(memory_space=pltpu.SMEM),
        pl.BlockSpec((1, tile), lambda t, place: (0, t)),
        pl.BlockSpec((virs, 1), lambda t, place: (0, 0)),
    ]
    in_specs += [pl.BlockSpec((depth, width), lambda t, place: (0, 0))] * len(leaders)
    operands = list(leaders)
    if bases is not None:
        in_specs += [flat] * len(bases)
        operands += bases
    for (_, start, stop), (exact, received, offset) in zip(spans, sums):
        spec = pl.BlockSpec((1, stop - start, tile), functools.partial(lambda offset, t, place: (offset, 0, t), offset))
        in_specs += [spec, spec]
        operands += [exact, received]
    out_shape = [jax.ShapeDtypeStruct((depth, virs), kind) for kind in out_types]
    out_specs = [flat] * len(leaders)
    aliases = {}
    if whole is not None:
        out_shape[0] = jax.ShapeDtypeStruct(whole, out_types[0])
        out_specs[0] = pl.BlockSpec((1, depth, tile), lambda t, place: (place[OWN] + orbital, 0, t))
        if previous is not None:
            in_specs.append(pl.BlockSpec(memory_space=pl.ANY))
            operands.append(previous)
            aliases = {4 + len(operands) - 1: 0}
    return pl.pallas_call(
        functools.partial(gamma_kernel, spans, orbital, len(leaders), bases is not None),
        grid_spec=pltpu.PrefetchScalarGridSpec(
            num_scalar_prefetch=1,
            grid=(virs // tile,),
            in_specs=in_specs,
            out_specs=out_specs,
            scratch_shapes=[pltpu.VMEM((width, tile), jnp.bfloat16)],
        ),
        out_shape=out_shape,
        input_output_aliases=aliases,
        compiler_params=params(),
        cost_estimate=BRIEF,
    )(place, energies, row, column, *operands)


def shards(orbital_b, occ_energy, vir_energy):
    occ_index = lax.axis_index("occ")
    aux_index = lax.axis_index("aux")
    occ_count = lax.axis_size("occ")
    aux_count = lax.axis_size("aux")
    chips = aux_count // 2
    rows, depth, virs = orbital_b.shape
    half = rows // 2
    core = aux_index % 2

    def to_mate(value):
        return lax.ppermute(value, "aux", [(at, at ^ 1) for at in range(aux_count)])

    def to_chip(value):
        return lax.ppermute(value, "aux", [(at, (at + 2) % aux_count) for at in range(aux_count)])

    place = jnp.stack([
        core * half,
        (1 - core) * half,
        occ_index * rows + core * half,
        jnp.maximum(occ_index - 1, 0) * rows,
        jnp.minimum(occ_index + 1, occ_count - 1) * rows,
    ]).astype(jnp.int32)

    unit = virs // 3
    spans = [(partner, start, start + unit) for partner in (0, 1) for start in range(0, virs, unit)]
    groups = [(0, half // 2), (half // 2, half - half // 2)]

    near, far = [], []

    def bring(after):
        partner, start, stop = spans[len(near)]
        columns = orbital_b[0, :, start:stop] if after is None else leader_columns(orbital_b, start, stop, after)
        near.append(shifted(columns, "occ", 1 - 2 * partner))
        far.append(to_mate(near[-1]))
        return columns

    columns = bring(None)
    fetched = [
        to_mate(mate_orbitals(place, orbital_b, *group, after)) for group, after in zip(groups, (columns, near[0]))
    ]

    steps = [(piece, *group) for piece in range(4) for group in groups]
    steps += [(4, *groups[0]), (5, *groups[0]), (4, *groups[1])] + [(5, at, 1) for at in range(half // 2, half)]
    brings = (0, 2, 4, 6, 7)
    ahead = 2 if chips == 2 else 1
    fixed = (place, occ_energy, vir_energy[None, :], vir_energy[:, None])
    narrow = orbital_b.dtype
    arrived, found, bases = [], {}, []
    rounded = vir_energy

    def gamma(leaders, pieces, orbital, **more):
        parts, sums = zip(*[found[piece, orbital] for piece in pieces])
        return gamma_rows(*fixed, leaders, parts, orbital, sums, **more)

    for at, (piece, first, count) in enumerate(steps):
        after = [arrived[at - ahead] if at >= ahead else vir_energy, rounded]
        if at == 9:
            early = [jnp.concatenate(pieces[:4], axis=1) for pieces in (near, far)]
        for orbital in range(half):
            if at == (9, 9, 10, 11)[4 * orbital // half]:
                bases.append(gamma(early, range(4), orbital, out_types=[jnp.float32] * 2))
                after.append(bases[-1][0])
        group = min(1, first // groups[1][0])
        exact, rounded = partial_integrals(
            place, near[piece].T, far[piece].T, orbital_b, fetched[group], first, count, first - groups[group][0], after
        )
        received = to_chip(rounded) if chips > 1 else jnp.zeros_like(rounded)
        for _ in range(chips - 2):
            exact = exact + received.astype(jnp.float32)
            received = to_chip(received)
        arrived.append(received if chips <= 2 else exact)
        if at in brings:
            bring(rounded)
        for offset in range(count):
            found[piece, first + offset] = (spans[piece], (exact, received, offset))

    late = [jnp.concatenate(pieces[4:], axis=1) for pieces in (near, far)]
    out, owed = None, []

    def returned(out):
        orbital, value = owed.pop(0)
        return lax.dynamic_update_slice_in_dim(out, value[None], (1 - core) * half + orbital, 0)

    for orbital in range(half // 2):
        out, other = gamma(
            late, (4, 5), orbital, bases=bases[orbital], out_types=[narrow] * 2, whole=orbital_b.shape, previous=out
        )
        owed.append((orbital, to_mate(other)))
    for orbital in range(half // 2, half):
        sofar = gamma([near[4], far[4]], (4,), orbital, bases=bases[orbital], out_types=[jnp.float32] * 2)
        (other,) = gamma(far[5:], (5,), orbital, bases=sofar[1:], out_types=[narrow], tile=virs)
        owed.append((orbital, to_mate(other)))
        if orbital == half - 1:
            out = returned(out)
        (out,) = gamma(
            near[5:], (5,), orbital, bases=sofar[:1], out_types=[narrow], tile=virs,
            whole=orbital_b.shape, previous=out,
        )
        while len(owed) > 2:
            out = returned(out)
    while owed:
        out = returned(out)
    return out


def solution(mesh):
    placed = (P("occ", "aux", None), P(), P())
    return jax.shard_map(
        shards, mesh=mesh, in_specs=placed, out_specs=P("occ", "aux", None), check_vma=False
    )
```

```python
import functools

import jax
import jax.numpy as jnp
from jax import lax
from jax.experimental import pallas as pl
from jax.experimental.pallas import tpu as pltpu
from jax.sharding import PartitionSpec as P

VMEM_BYTES = 56 * 1024 * 1024

BRIEF = pl.CostEstimate(flops=0, bytes_accessed=0, transcendentals=0)

OWN, OWN_ENERGY, PARTNER_ENERGY = 0, 1, 2


def shifted(value, axis, steps):
    count = lax.axis_size(axis)
    initial, last = (max(0, -steps), min(count, count - steps))
    return lax.ppermute(value, axis, [(source, source + steps) for source in range(initial, last)])


def params():
    return pltpu.CompilerParams(vmem_limit_bytes=VMEM_BYTES)


def columns_kernel(source, after, out):
    out[...] = source[0]


def leader_columns(orbital_b, start, stop, after):
    depth = orbital_b.shape[1]
    width = 128 if (start % 128 == 0 and stop % 128 == 0) else stop - start
    return pl.pallas_call(
        columns_kernel,
        grid=((stop - start) // width,),
        in_specs=[
            pl.BlockSpec((1, depth, width), lambda t: (0, 0, start // width + t)),
            pl.BlockSpec(memory_space=pl.ANY),
        ],
        out_specs=pl.BlockSpec((depth, width), lambda t: (0, t)),
        out_shape=jax.ShapeDtypeStruct((depth, stop - start), orbital_b.dtype),
        compiler_params=params(),
        cost_estimate=BRIEF,
    )(orbital_b, after)


def partial_kernel(place, near, far, near_b, far_b, *refs):
    exact, rounded = refs[-2:]
    total = jnp.dot(near[...], near_b[0], preferred_element_type=jnp.float32)
    total += jnp.dot(far[...], far_b[0], preferred_element_type=jnp.float32)
    exact[0] = total
    rounded[0] = total.astype(jnp.bfloat16)


def partial_integrals(place, near, far, orbital_b, fetched, first, count, left, right, after):
    width, depth = near.shape
    virs = orbital_b.shape[2]
    tile = right - left if (right - left) == virs or left % 128 else virs // 3
    begin = left // tile
    grid_spec = pltpu.PrefetchScalarGridSpec(
        num_scalar_prefetch=1,
        grid=(count, (right - left) // tile),
        in_specs=[
            pl.BlockSpec((width, depth), lambda i, t, place: (0, 0)),
            pl.BlockSpec((width, depth), lambda i, t, place: (0, 0)),
            pl.BlockSpec((1, depth, tile), lambda i, t, place: (place[OWN] + first + i, 0, begin + t)),
            pl.BlockSpec((1, depth, tile), lambda i, t, place: (place[OWN] + first + i, 0, begin + t)),
        ] + [pl.BlockSpec(memory_space=pl.ANY)] * len(after),
        out_specs=[pl.BlockSpec((1, width, tile), lambda i, t, place: (i, 0, t))] * 2,
    )
    return pl.pallas_call(
        partial_kernel,
        grid_spec=grid_spec,
        out_shape=[
            jax.ShapeDtypeStruct((count, width, right - left), jnp.float32),
            jax.ShapeDtypeStruct((count, width, right - left), jnp.bfloat16),
        ],
        compiler_params=params(),
        cost_estimate=BRIEF,
    )(place, near, far, orbital_b, fetched, *after)


def gamma_kernel(spans, orbital, place, energies, row, column, near, far, *refs):
    own, upper, lower, amplitude = refs[-4:]
    own_energy = energies[place[OWN_ENERGY] + orbital]
    at = 0
    for index, parts in enumerate(spans):
        exact, received = refs[2 * index], refs[2 * index + 1]
        lowest = 0
        for partner, start, stop in parts:
            here = slice(lowest, lowest + stop - start)
            denominator = (row[...] + column[start:stop]) - own_energy - energies[place[PARTNER_ENERGY + partner]]
            integral = exact[0, here] + received[0, here].astype(jnp.float32)
            amplitude[at : at + stop - start] = (integral / denominator).astype(jnp.bfloat16)
            lowest += stop - start
            at += stop - start
    own[0] = jnp.dot(near[...], amplitude[...], preferred_element_type=jnp.float32).astype(own.dtype)
    other = jnp.dot(far[...], amplitude[...], preferred_element_type=jnp.float32).astype(upper.dtype)
    upper[...] = other[: upper.shape[0]]
    lower[...] = other[upper.shape[0] :]


def gamma_rows(place, energies, row, column, near, far, orbital, left, right, sums, whole, previous):
    depth, width = near.shape
    virs = row.shape[1]
    tile = virs // 3
    begin = left // tile
    in_specs = [
        pl.BlockSpec(memory_space=pltpu.SMEM),
        pl.BlockSpec((1, tile), lambda t, place: (0, begin + t)),
        pl.BlockSpec((virs, 1), lambda t, place: (0, 0)),
        pl.BlockSpec((depth, width), lambda t, place: (0, 0)),
        pl.BlockSpec((depth, width), lambda t, place: (0, 0)),
    ]
    operands = []
    for spans, exact, received, offset, lowest in sums:
        shift = begin - lowest // tile
        spec = pl.BlockSpec(
            (1, exact.shape[1], tile),
            functools.partial(lambda offset, shift, t, place: (offset, 0, shift + t), offset, shift),
        )
        in_specs += [spec, spec]
        operands += [exact, received]
    aliases = {}
    if previous is not None:
        in_specs.append(pl.BlockSpec(memory_space=pl.ANY))
        operands.append(previous)
        aliases = {6 + len(operands) - 1: 0}
    return pl.pallas_call(
        functools.partial(gamma_kernel, [spans for spans, *_ in sums], orbital),
        grid_spec=pltpu.PrefetchScalarGridSpec(
            num_scalar_prefetch=1,
            grid=((right - left) // tile,),
            in_specs=in_specs,
            out_specs=[
                pl.BlockSpec((1, depth, tile), lambda t, place: (place[OWN] + orbital, 0, begin + t)),
            ] + [pl.BlockSpec((depth // 2, tile), lambda t, place: (0, t))] * 2,
            scratch_shapes=[pltpu.VMEM((width, tile), jnp.bfloat16)],
        ),
        out_shape=[
            jax.ShapeDtypeStruct(whole.shape, whole.dtype),
        ] + [jax.ShapeDtypeStruct((depth // 2, right - left), whole.dtype)] * 2,
        input_output_aliases=aliases,
        compiler_params=params(),
        cost_estimate=BRIEF,
    )(place, energies, row, column, near, far, *operands)


def shards(orbital_b, occ_energy, vir_energy):
    occ_index = lax.axis_index("occ")
    aux_index = lax.axis_index("aux")
    occ_count = lax.axis_size("occ")
    aux_count = lax.axis_size("aux")
    chips = aux_count // 2
    rows, depth, virs = orbital_b.shape
    half = rows // 2
    core = aux_index % 2

    def to_mate(value):
        return lax.ppermute(value, "aux", [(at, at ^ 1) for at in range(aux_count)])

    def to_chip(value):
        return lax.ppermute(value, "aux", [(at, (at + 2) % aux_count) for at in range(aux_count)])

    place = jnp.stack([
        core * half,
        occ_index * rows + core * half,
        jnp.maximum(occ_index - 1, 0) * rows,
        jnp.minimum(occ_index + 1, occ_count - 1) * rows,
    ]).astype(jnp.int32)

    unit = virs // 3
    spans = [(partner, start, start + unit) for partner in (0, 1) for start in range(0, virs, unit)]
    groups = [(0, half // 2), (half // 2, half - half // 2)]

    near, far = [], []

    def bring(after):
        partner, start, stop = spans[len(near)]
        columns = orbital_b[0, :, start:stop] if after is None else leader_columns(orbital_b, start, stop, after)
        near.append(shifted(columns, "occ", 1 - 2 * partner))
        far.append(to_mate(near[-1]))
        return columns

    bring(None)
    fetched = to_mate(orbital_b)

    steps = [((piece,), *group, 0, virs) for piece in range(4) for group in groups]
    steps += [((4, 5), at, 1, 0, virs) for at in range(half - 1)]
    steps += [((4, 5), half - 1, 1, *ends) for ends in ((0, 2 * unit), (2 * unit, virs))]
    brings = {0: 1, 2: 1, 4: 1, 6: 2}
    ahead = 2 if chips == 2 else 1
    arrived, turned, found = [], {}, [[] for _ in range(half)]
    rounded = vir_energy
    for at, (pieces, first, count, left, right) in enumerate(steps):
        if pieces not in turned:
            turned[pieces] = [jnp.concatenate([side[piece] for piece in pieces], axis=1).T for side in (near, far)]
        after = [arrived[at - ahead] if at >= ahead else vir_energy, rounded]
        exact, rounded = partial_integrals(
            place, *turned[pieces], orbital_b, fetched, first, count, left, right, after
        )
        received = to_chip(rounded) if chips > 1 else jnp.zeros_like(rounded)
        for _ in range(chips - 2):
            exact = exact + received.astype(jnp.float32)
            received = to_chip(received)
        arrived.append(received if chips <= 2 else exact)
        for _ in range(brings.get(at, 0)):
            bring(rounded if at else None)
        for offset in range(count):
            found[first + offset].append(([spans[piece] for piece in pieces], exact, received, offset, left))

    leaders = [jnp.concatenate(side, axis=1) for side in (near, far)]
    row, column = vir_energy[None, :], vir_energy[:, None]
    out, owed = None, []
    for orbital in range(half):
        ends = [(0, virs)] if orbital < half - 1 else [(0, 2 * unit), (2 * unit, virs)]
        for left, right in ends:
            sums = found[orbital][:4] + [entry for entry in found[orbital][4:] if entry[-1] == left]
            out, upper, lower = gamma_rows(
                place, occ_energy, row, column, *leaders, orbital, left, right, sums, orbital_b, out
            )
            owed.append((to_mate(upper), to_mate(lower), orbital, left))
            if len(owed) > 1:
                out = put(out, *owed.pop(0), (1 - core) * half)
    return put(out, *owed.pop(0), (1 - core) * half)


def put(out, upper, lower, orbital, left, offset):
    zero = jnp.zeros((), jnp.int32)
    out = lax.dynamic_update_slice(out, upper[None], (offset + orbital, zero, zero + left))
    return lax.dynamic_update_slice(out, lower[None], (offset + orbital, zero + upper.shape[0], zero + left))


def solution(mesh):
    placed = (P("occ", "aux", None), P(), P())
    return jax.shard_map(
        shards, mesh=mesh, in_specs=placed, out_specs=P("occ", "aux", None), check_vma=False
    )
```

```python
import functools

import jax
import jax.numpy as jnp
from jax import lax
from jax.experimental import pallas as pl
from jax.experimental.pallas import tpu as pltpu
from jax.sharding import PartitionSpec as P

VMEM_BYTES = 56 * 1024 * 1024

PARTS = 3

BRIEF = pl.CostEstimate(flops=0, bytes_accessed=0, transcendentals=0)

OWN, OWN_ENERGY, PARTNER_ENERGY = 0, 1, 2


def shifted(value, axis, steps):
    count = lax.axis_size(axis)
    initial, last = (max(0, -steps), min(count, count - steps))
    return lax.ppermute(value, axis, [(source, source + steps) for source in range(initial, last)])


def params():
    return pltpu.CompilerParams(vmem_limit_bytes=VMEM_BYTES)


def columns_kernel(source, after, out):
    out[...] = source[0]


def leader_columns(orbital_b, start, stop, after):
    depth = orbital_b.shape[1]
    width = 128 if (start % 128 == 0 and stop % 128 == 0) else stop - start
    return pl.pallas_call(
        columns_kernel,
        grid=((stop - start) // width,),
        in_specs=[
            pl.BlockSpec((1, depth, width), lambda t: (0, 0, start // width + t)),
            pl.BlockSpec(memory_space=pl.ANY),
        ],
        out_specs=pl.BlockSpec((depth, width), lambda t: (0, t)),
        out_shape=jax.ShapeDtypeStruct((depth, stop - start), orbital_b.dtype),
        compiler_params=params(),
        cost_estimate=BRIEF,
    )(orbital_b, after)


def partial_kernel(place, near, far, near_b, far_b, *refs):
    exact, rounded = refs[-2:]
    total = jnp.dot(near[...], near_b[0], preferred_element_type=jnp.float32)
    total += jnp.dot(far[...], far_b[0], preferred_element_type=jnp.float32)
    exact[0] = total
    rounded[0] = total.astype(jnp.bfloat16)


def partial_integrals(place, near, far, orbital_b, fetched, first, count, left, right, after):
    width, depth = near.shape
    virs = orbital_b.shape[2]
    tile = right - left if (right - left) == virs or left % 128 else virs // 3
    begin = left // tile
    grid_spec = pltpu.PrefetchScalarGridSpec(
        num_scalar_prefetch=1,
        grid=(count, (right - left) // tile),
        in_specs=[
            pl.BlockSpec((width, depth), lambda i, t, place: (0, 0)),
            pl.BlockSpec((width, depth), lambda i, t, place: (0, 0)),
            pl.BlockSpec((1, depth, tile), lambda i, t, place: (place[OWN] + first + i, 0, begin + t)),
            pl.BlockSpec((1, depth, tile), lambda i, t, place: (place[OWN] + first + i, 0, begin + t)),
        ] + [pl.BlockSpec(memory_space=pl.ANY)] * len(after),
        out_specs=[pl.BlockSpec((1, width, tile), lambda i, t, place: (i, 0, t))] * 2,
    )
    return pl.pallas_call(
        partial_kernel,
        grid_spec=grid_spec,
        out_shape=[
            jax.ShapeDtypeStruct((count, width, right - left), jnp.float32),
            jax.ShapeDtypeStruct((count, width, right - left), jnp.bfloat16),
        ],
        compiler_params=params(),
        cost_estimate=BRIEF,
    )(place, near, far, orbital_b, fetched, *after)


def gamma_kernel(spans, orbital, place, energies, row, column, near, far, *refs):
    outs, amplitude = refs[-1 - PARTS :-1], refs[-1]
    own = refs[-2 - PARTS]
    own_energy = energies[place[OWN_ENERGY] + orbital]
    at = 0
    for index, parts in enumerate(spans):
        exact, received = refs[2 * index], refs[2 * index + 1]
        lowest = 0
        for partner, start, stop in parts:
            here = slice(lowest, lowest + stop - start)
            denominator = (row[...] + column[start:stop]) - own_energy - energies[place[PARTNER_ENERGY + partner]]
            integral = exact[0, here] + received[0, here].astype(jnp.float32)
            amplitude[at : at + stop - start] = (integral / denominator).astype(jnp.bfloat16)
            lowest += stop - start
            at += stop - start
    own[0] = jnp.dot(near[...], amplitude[...], preferred_element_type=jnp.float32).astype(own.dtype)
    other = jnp.dot(far[...], amplitude[...], preferred_element_type=jnp.float32).astype(own.dtype)
    rows = other.shape[0] // PARTS
    for part, out in enumerate(outs):
        out[...] = other[part * rows : (part + 1) * rows]


def gamma_rows(place, energies, row, column, near, far, orbital, left, right, sums, whole, previous, after):
    depth, width = near.shape
    virs = row.shape[1]
    tile = virs // 3
    begin = left // tile
    in_specs = [
        pl.BlockSpec(memory_space=pltpu.SMEM),
        pl.BlockSpec((1, tile), lambda t, place: (0, begin + t)),
        pl.BlockSpec((virs, 1), lambda t, place: (0, 0)),
        pl.BlockSpec((depth, width), lambda t, place: (0, 0)),
        pl.BlockSpec((depth, width), lambda t, place: (0, 0)),
    ]
    operands = []
    for spans, exact, received, offset, lowest in sums:
        shift = begin - lowest // tile
        spec = pl.BlockSpec(
            (1, exact.shape[1], tile),
            functools.partial(lambda offset, shift, t, place: (offset, 0, shift + t), offset, shift),
        )
        in_specs += [spec, spec]
        operands += [exact, received]
    aliases = {}
    if previous is not None:
        in_specs.append(pl.BlockSpec(memory_space=pl.ANY))
        operands.append(previous)
        aliases = {6 + len(operands) - 1: 0}
    in_specs += [pl.BlockSpec(memory_space=pl.ANY)] * len(after)
    operands += after
    return pl.pallas_call(
        functools.partial(gamma_kernel, [spans for spans, *_ in sums], orbital),
        grid_spec=pltpu.PrefetchScalarGridSpec(
            num_scalar_prefetch=1,
            grid=((right - left) // tile,),
            in_specs=in_specs,
            out_specs=[
                pl.BlockSpec((1, depth, tile), lambda t, place: (place[OWN] + orbital, 0, begin + t)),
            ] + [pl.BlockSpec((depth // PARTS, tile), lambda t, place: (0, t))] * PARTS,
            scratch_shapes=[pltpu.VMEM((width, tile), jnp.bfloat16)],
        ),
        out_shape=[
            jax.ShapeDtypeStruct(whole.shape, whole.dtype),
        ] + [jax.ShapeDtypeStruct((depth // PARTS, right - left), whole.dtype)] * PARTS,
        input_output_aliases=aliases,
        compiler_params=params(),
        cost_estimate=BRIEF,
    )(place, energies, row, column, near, far, *operands)


def shards(orbital_b, occ_energy, vir_energy):
    occ_index = lax.axis_index("occ")
    aux_index = lax.axis_index("aux")
    occ_count = lax.axis_size("occ")
    aux_count = lax.axis_size("aux")
    chips = aux_count // 2
    rows, depth, virs = orbital_b.shape
    half = rows // 2
    core = aux_index % 2

    def to_mate(value):
        return lax.ppermute(value, "aux", [(at, at ^ 1) for at in range(aux_count)])

    def to_chip(value):
        return lax.ppermute(value, "aux", [(at, (at + 2) % aux_count) for at in range(aux_count)])

    place = jnp.stack([
        core * half,
        occ_index * rows + core * half,
        jnp.maximum(occ_index - 1, 0) * rows,
        jnp.minimum(occ_index + 1, occ_count - 1) * rows,
    ]).astype(jnp.int32)

    unit = virs // 3
    spans = [(partner, start, start + unit) for partner in (0, 1) for start in range(0, virs, unit)]
    groups = [(0, half // 2), (half // 2, half - half // 2)]

    near, far = [], []

    def bring(after):
        partner, start, stop = spans[len(near)]
        columns = orbital_b[0, :, start:stop] if after is None else leader_columns(orbital_b, start, stop, after)
        near.append(shifted(columns, "occ", 1 - 2 * partner))
        far.append(to_mate(near[-1]))
        return columns

    bring(None)
    fetched = to_mate(orbital_b)

    steps = [((piece,), *group, 0, virs) for piece in range(4) for group in groups]
    steps += [((4, 5), at, 1, 0, virs) for at in range(half - 1)]
    steps += [((4, 5), half - 1, 1, *ends) for ends in ((0, 2 * unit), (2 * unit, virs))]
    brings = {0: 1, 2: 1, 4: 1, 5: 1, 6: 1}
    ahead = 2 if chips == 2 else 1
    arrived, sent, turned, found = [], [], {}, [[] for _ in range(half)]
    rounded = vir_energy
    for at, (pieces, first, count, left, right) in enumerate(steps):
        if pieces not in turned:
            turned[pieces] = [jnp.concatenate([side[piece] for piece in pieces], axis=1).T for side in (near, far)]
        lead = ahead + (at >= 9 and chips == 2)
        after = [arrived[at - lead] if at >= lead else vir_energy, rounded]
        exact, rounded = partial_integrals(
            place, *turned[pieces], orbital_b, fetched, first, count, left, right, after
        )
        received = to_chip(rounded) if chips > 1 else jnp.zeros_like(rounded)
        for _ in range(chips - 2):
            exact = exact + received.astype(jnp.float32)
            received = to_chip(received)
        arrived.append(received if chips <= 2 else exact)
        sent.append(rounded)
        for _ in range(brings.get(at, 0)):
            bring(rounded if at else None)
        for offset in range(count):
            found[first + offset].append(([spans[piece] for piece in pieces], exact, received, offset, left))

    leaders = [jnp.concatenate(side, axis=1) for side in (near, far)]
    row, column = vir_energy[None, :], vir_energy[:, None]
    out, owed = None, []
    for orbital in range(half):
        ends = [(0, virs)] if orbital < half - 1 else [(0, 2 * unit), (2 * unit, virs)]
        for left, right in ends:
            sums = found[orbital][:4] + [entry for entry in found[orbital][4:] if entry[-1] == left]
            out, *others = gamma_rows(
                place, occ_energy, row, column, *leaders, orbital, left, right, sums, orbital_b, out, sent[(10, 12)[orbital] :][:1] if orbital < 2 else [],
            )
            owed.append(([to_mate(other) for other in others], orbital, left))
            if len(owed) > 1:
                out = put(out, *owed.pop(0), (1 - core) * half)
    return put(out, *owed.pop(0), (1 - core) * half)


def put(out, parts, orbital, left, offset):
    zero = jnp.zeros((), jnp.int32)
    for part, value in enumerate(parts):
        out = lax.dynamic_update_slice(out, value[None], (offset + orbital, zero + part * value.shape[0], zero + left))
    return out


def solution(mesh):
    placed = (P("occ", "aux", None), P(), P())
    return jax.shard_map(
        shards, mesh=mesh, in_specs=placed, out_specs=P("occ", "aux", None), check_vma=False
    )
```

```python
import functools

import jax
import jax.numpy as jnp
from jax import lax
from jax.experimental import pallas as pl
from jax.experimental.pallas import tpu as pltpu
from jax.sharding import PartitionSpec as P

VMEM_BYTES = 56 * 1024 * 1024

BRIEF = pl.CostEstimate(flops=0, bytes_accessed=0, transcendentals=0)

OWN, OWN_ENERGY, PARTNER_ENERGY = 0, 1, 2


def shifted(value, axis, steps):
    count = lax.axis_size(axis)
    initial, last = (max(0, -steps), min(count, count - steps))
    return lax.ppermute(value, axis, [(source, source + steps) for source in range(initial, last)])


def params():
    return pltpu.CompilerParams(vmem_limit_bytes=VMEM_BYTES)


def columns_kernel(source, after, out):
    out[...] = source[0]


def leader_columns(orbital_b, start, stop, after):
    depth = orbital_b.shape[1]
    width = 128 if (start % 128 == 0 and stop % 128 == 0) else stop - start
    return pl.pallas_call(
        columns_kernel,
        grid=((stop - start) // width,),
        in_specs=[
            pl.BlockSpec((1, depth, width), lambda t: (0, 0, start // width + t)),
            pl.BlockSpec(memory_space=pl.ANY),
        ],
        out_specs=pl.BlockSpec((depth, width), lambda t: (0, t)),
        out_shape=jax.ShapeDtypeStruct((depth, stop - start), orbital_b.dtype),
        compiler_params=params(),
        cost_estimate=BRIEF,
    )(orbital_b, after)


def partial_kernel(pieces, place, *refs):
    near_b, far_b = refs[2 * pieces : 2 * pieces + 2]
    exact, rounded = refs[-2:]
    at = 0
    for piece in range(pieces):
        near, far = refs[2 * piece : 2 * piece + 2]
        total = jnp.dot(near[...], near_b[0], preferred_element_type=jnp.float32)
        total += jnp.dot(far[...], far_b[0], preferred_element_type=jnp.float32)
        here = slice(at, at + near.shape[0])
        exact[0, here] = total
        rounded[0, here] = total.astype(jnp.bfloat16)
        at += near.shape[0]


def partial_integrals(place, leaders, orbital_b, fetched, first, count, left, right, after):
    depth, virs = orbital_b.shape[1:]
    width = sum(near.shape[0] for near, _ in leaders)
    tile = right - left if (right - left) == virs or left % 128 else virs // 3
    begin = left // tile
    own = pl.BlockSpec((1, depth, tile), lambda i, t, place: (place[OWN] + first + i, 0, begin + t))
    grid_spec = pltpu.PrefetchScalarGridSpec(
        num_scalar_prefetch=1,
        grid=(count, (right - left) // tile),
        in_specs=[pl.BlockSpec(side.shape, lambda i, t, place: (0, 0)) for pair in leaders for side in pair]
        + [own, own] + [pl.BlockSpec(memory_space=pl.ANY)] * len(after),
        out_specs=[pl.BlockSpec((1, width, tile), lambda i, t, place: (i, 0, t))] * 2,
    )
    return pl.pallas_call(
        functools.partial(partial_kernel, len(leaders)),
        grid_spec=grid_spec,
        out_shape=[
            jax.ShapeDtypeStruct((count, width, right - left), jnp.float32),
            jax.ShapeDtypeStruct((count, width, right - left), jnp.bfloat16),
        ],
        compiler_params=params(),
        cost_estimate=BRIEF,
    )(place, *[side for pair in leaders for side in pair], orbital_b, fetched, *after)


def gamma_kernel(spans, orbital, widths, parts, place, energies, row, column, *refs):
    pieces, sums = refs[: 2 * len(widths)], refs[2 * len(widths) :]
    own, outs = refs[-5 - parts], refs[-4 - parts : -4]
    amplitude, near, far, arrived = refs[-4:]
    copies = []
    for side, whole in enumerate((near, far)):
        at = 0
        for index, width in enumerate(widths):
            which = side * len(widths) + index
            copies.append(pltpu.make_async_copy(pieces[which], whole.at[:, at : at + width], arrived.at[which]))
            at += width

    @pl.when(pl.program_id(0) == 0)
    def _():
        for copy in copies:
            copy.start()

    own_energy = energies[place[OWN_ENERGY] + orbital]
    at = 0
    for index, ranges in enumerate(spans):
        exact, received = sums[2 * index], sums[2 * index + 1]
        lowest = 0
        for partner, start, stop in ranges:
            here = slice(lowest, lowest + stop - start)
            denominator = (row[...] + column[start:stop]) - own_energy - energies[place[PARTNER_ENERGY + partner]]
            integral = exact[0, here] + received[0, here].astype(jnp.float32)
            amplitude[at : at + stop - start] = (integral / denominator).astype(jnp.bfloat16)
            lowest += stop - start
            at += stop - start

    @pl.when(pl.program_id(0) == 0)
    def _():
        for copy in copies:
            copy.wait()

    other = jnp.dot(far[...], amplitude[...], preferred_element_type=jnp.float32).astype(own.dtype)
    rows = other.shape[0] // parts
    for part, out in enumerate(outs):
        out[...] = other[part * rows : (part + 1) * rows]
    own[0] = jnp.dot(near[...], amplitude[...], preferred_element_type=jnp.float32).astype(own.dtype)


def gamma_rows(place, energies, row, column, near, far, orbital, left, right, sums, whole, previous, after):
    depth = near[0].shape[0]
    widths = [piece.shape[1] for piece in near]
    width = sum(widths)
    virs = row.shape[1]
    tile = virs // 3
    begin = left // tile
    parts = next(count for count in (3, 2, 1) if depth % (16 * count) == 0 or count == 1)
    in_specs = [
        pl.BlockSpec(memory_space=pltpu.SMEM),
        pl.BlockSpec((1, tile), lambda t, place: (0, begin + t)),
        pl.BlockSpec((virs, 1), lambda t, place: (0, 0)),
    ] + [pl.BlockSpec(memory_space=pl.ANY)] * (2 * len(widths))
    operands = [place, energies, row, column, *near, *far]
    for spans, exact, received, offset, lowest in sums:
        shift = begin - lowest // tile
        spec = pl.BlockSpec(
            (1, exact.shape[1], tile),
            functools.partial(lambda offset, shift, t, place: (offset, 0, shift + t), offset, shift),
        )
        in_specs += [spec, spec]
        operands += [exact, received]
    aliases = {}
    if previous is not None:
        aliases = {len(operands): 0}
        operands.append(previous)
    operands += after
    in_specs += [pl.BlockSpec(memory_space=pl.ANY)] * (len(operands) - 1 - len(in_specs))
    return pl.pallas_call(
        functools.partial(gamma_kernel, [spans for spans, *_ in sums], orbital, widths, parts),
        grid_spec=pltpu.PrefetchScalarGridSpec(
            num_scalar_prefetch=1,
            grid=((right - left) // tile,),
            in_specs=in_specs,
            out_specs=[
                pl.BlockSpec((1, depth, tile), lambda t, place: (place[OWN] + orbital, 0, begin + t)),
            ] + [pl.BlockSpec((depth // parts, tile), lambda t, place: (0, t))] * parts,
            scratch_shapes=[
                pltpu.VMEM((width, tile), jnp.bfloat16),
                pltpu.VMEM((depth, width), jnp.bfloat16),
                pltpu.VMEM((depth, width), jnp.bfloat16),
                pltpu.SemaphoreType.DMA((2 * len(widths),)),
            ],
        ),
        out_shape=[
            jax.ShapeDtypeStruct(whole.shape, whole.dtype),
        ] + [jax.ShapeDtypeStruct((depth // parts, right - left), whole.dtype)] * parts,
        input_output_aliases=aliases,
        compiler_params=params(),
        cost_estimate=BRIEF,
    )(*operands)


def shards(orbital_b, occ_energy, vir_energy):
    occ_index = lax.axis_index("occ")
    aux_index = lax.axis_index("aux")
    occ_count = lax.axis_size("occ")
    aux_count = lax.axis_size("aux")
    chips = aux_count // 2
    rows, depth, virs = orbital_b.shape
    half = rows // 2
    core = aux_index % 2

    def to_mate(value):
        return lax.ppermute(value, "aux", [(at, at ^ 1) for at in range(aux_count)])

    def to_chip(value):
        return lax.ppermute(value, "aux", [(at, (at + 2) % aux_count) for at in range(aux_count)])

    place = jnp.stack([
        core * half,
        occ_index * rows + core * half,
        jnp.maximum(occ_index - 1, 0) * rows,
        jnp.minimum(occ_index + 1, occ_count - 1) * rows,
    ]).astype(jnp.int32)

    unit = virs // 3
    spans = [(partner, start, start + unit) for partner in (0, 1) for start in range(0, virs, unit)]
    groups = [(0, half // 2), (half // 2, half - half // 2)]

    near, far = [], []

    def bring(after):
        partner, start, stop = spans[len(near)]
        columns = orbital_b[0, :, start:stop] if after is None else leader_columns(orbital_b, start, stop, after)
        near.append(shifted(columns, "occ", 1 - 2 * partner))
        far.append(to_mate(near[-1]))
        return columns

    bring(None)
    fetched = to_mate(orbital_b)

    steps = [((piece,), *group, 0, virs) for piece in range(4) for group in groups]
    steps += [((4, 5), at, 1, 0, virs) for at in range(half - 1)]
    steps += [((4, 5), half - 1, 1, *ends) for ends in ((0, 2 * unit), (2 * unit, virs))]
    brings = {0: 1, 2: 1, 4: 1, 5: 1, 6: 1}
    ahead = 2 if chips == 2 else 1
    arrived, sent, turned, found = [], [], {}, [[] for _ in range(half)]
    rounded = vir_energy
    for at, (pieces, first, count, left, right) in enumerate(steps):
        for piece in pieces:
            if piece not in turned:
                turned[piece] = near[piece].T, far[piece].T
        lead = ahead + (at >= 9 and chips == 2)
        after = [arrived[at - lead] if at >= lead else vir_energy, rounded]
        exact, rounded = partial_integrals(
            place, [turned[piece] for piece in pieces], orbital_b, fetched, first, count, left, right, after
        )
        received = to_chip(rounded) if chips > 1 else jnp.zeros_like(rounded)
        for _ in range(chips - 2):
            exact = exact + received.astype(jnp.float32)
            received = to_chip(received)
        arrived.append(received if chips <= 2 else exact)
        sent.append(rounded)
        for _ in range(brings.get(at, 0)):
            bring(rounded if at else None)
        for offset in range(count):
            found[first + offset].append(([spans[piece] for piece in pieces], exact, received, offset, left))

    row, column = vir_energy[None, :], vir_energy[:, None]
    out, owed = None, []
    for orbital in range(half):
        ends = [(0, virs)] if orbital < half - 1 else [(0, 2 * unit), (2 * unit, virs)]
        for left, right in ends:
            sums = found[orbital][:4] + [entry for entry in found[orbital][4:] if entry[-1] == left]
            out, *others = gamma_rows(
                place, occ_energy, row, column, near, far, orbital, left, right, sums, orbital_b, out, sent[(10, 12)[orbital] :][:1] if orbital < 2 else [],
            )
            owed.append(([to_mate(other) for other in others], orbital, left))
            if len(owed) > 1:
                out = put(out, *owed.pop(0), (1 - core) * half)
    return put(out, *owed.pop(0), (1 - core) * half)


def put(out, parts, orbital, left, offset):
    zero = jnp.zeros((), jnp.int32)
    for part, value in enumerate(parts):
        out = lax.dynamic_update_slice(out, value[None], (offset + orbital, zero + part * value.shape[0], zero + left))
    return out


def solution(mesh):
    placed = (P("occ", "aux", None), P(), P())
    return jax.shard_map(
        shards, mesh=mesh, in_specs=placed, out_specs=P("occ", "aux", None), check_vma=False
    )
```

```python
import functools

import jax
import jax.numpy as jnp
from jax import lax
from jax.experimental import pallas as pl
from jax.experimental.pallas import tpu as pltpu
from jax.sharding import PartitionSpec as P

VMEM_BYTES = 56 * 1024 * 1024

BRIEF = pl.CostEstimate(flops=0, bytes_accessed=0, transcendentals=0)

OWN, OWN_ENERGY, PARTNER_ENERGY = 0, 1, 2


def shifted(value, axis, steps):
    count = lax.axis_size(axis)
    initial, last = (max(0, -steps), min(count, count - steps))
    return lax.ppermute(value, axis, [(source, source + steps) for source in range(initial, last)])


def params():
    return pltpu.CompilerParams(vmem_limit_bytes=VMEM_BYTES)


def columns_kernel(source, after, out):
    out[...] = source[0]


def leader_columns(orbital_b, start, stop, after):
    depth = orbital_b.shape[1]
    width = 128 if (start % 128 == 0 and stop % 128 == 0) else stop - start
    return pl.pallas_call(
        columns_kernel,
        grid=((stop - start) // width,),
        in_specs=[
            pl.BlockSpec((1, depth, width), lambda t: (0, 0, start // width + t)),
            pl.BlockSpec(memory_space=pl.ANY),
        ],
        out_specs=pl.BlockSpec((depth, width), lambda t: (0, t)),
        out_shape=jax.ShapeDtypeStruct((depth, stop - start), orbital_b.dtype),
        compiler_params=params(),
        cost_estimate=BRIEF,
    )(orbital_b, after)


def partial_kernel(pieces, place, *refs):
    near_b, far_b = refs[2 * pieces : 2 * pieces + 2]
    exact, rounded = refs[-2:]
    at = 0
    for piece in range(pieces):
        near, far = refs[2 * piece : 2 * piece + 2]
        total = jnp.dot(near[...], near_b[0], preferred_element_type=jnp.float32)
        total += jnp.dot(far[...], far_b[0], preferred_element_type=jnp.float32)
        here = slice(at, at + near.shape[0])
        exact[0, here] = total
        rounded[0, here] = total.astype(jnp.bfloat16)
        at += near.shape[0]


def partial_integrals(place, leaders, orbital_b, fetched, first, count, left, right, after):
    depth, virs = orbital_b.shape[1:]
    width = sum(near.shape[0] for near, _ in leaders)
    tile = right - left if (right - left) == virs or left % 128 else virs // 3
    begin = left // tile
    own = pl.BlockSpec((1, depth, tile), lambda i, t, place: (place[OWN] + first + i, 0, begin + t))
    grid_spec = pltpu.PrefetchScalarGridSpec(
        num_scalar_prefetch=1,
        grid=(count, (right - left) // tile),
        in_specs=[pl.BlockSpec(side.shape, lambda i, t, place: (0, 0)) for pair in leaders for side in pair]
        + [own, own] + [pl.BlockSpec(memory_space=pl.ANY)] * len(after),
        out_specs=[pl.BlockSpec((1, width, tile), lambda i, t, place: (i, 0, t))] * 2,
    )
    return pl.pallas_call(
        functools.partial(partial_kernel, len(leaders)),
        grid_spec=grid_spec,
        out_shape=[
            jax.ShapeDtypeStruct((count, width, right - left), jnp.float32),
            jax.ShapeDtypeStruct((count, width, right - left), jnp.bfloat16),
        ],
        compiler_params=params(),
        cost_estimate=BRIEF,
    )(place, *[side for pair in leaders for side in pair], orbital_b, fetched, *after)


def gamma_kernel(spans, orbital, parts, place, energies, row, column, near, far, *refs):
    own, outs, amplitude = refs[-2 - parts], refs[-1 - parts : -1], refs[-1]
    own_energy = energies[place[OWN_ENERGY] + orbital]
    at = 0
    for index, ranges in enumerate(spans):
        exact, received = refs[2 * index], refs[2 * index + 1]
        lowest = 0
        for partner, start, stop in ranges:
            here = slice(lowest, lowest + stop - start)
            denominator = (row[...] + column[start:stop]) - own_energy - energies[place[PARTNER_ENERGY + partner]]
            integral = exact[0, here] + received[0, here].astype(jnp.float32)
            amplitude[at : at + stop - start] = (integral / denominator).astype(jnp.bfloat16)
            lowest += stop - start
            at += stop - start
    own[0] = jnp.dot(near[...], amplitude[...], preferred_element_type=jnp.float32).astype(own.dtype)
    other = jnp.dot(far[...], amplitude[...], preferred_element_type=jnp.float32).astype(own.dtype)
    rows = other.shape[0] // parts
    for part, out in enumerate(outs):
        out[...] = other[part * rows : (part + 1) * rows]


def gamma_rows(place, energies, row, column, near, far, orbital, left, right, sums, whole, previous, after):
    depth, width = near.shape
    virs = row.shape[1]
    tile = virs // 3
    begin = left // tile
    parts = next(count for count in (3, 2, 1) if depth % (16 * count) == 0 or count == 1)
    in_specs = [
        pl.BlockSpec(memory_space=pltpu.SMEM),
        pl.BlockSpec((1, tile), lambda t, place: (0, begin + t)),
        pl.BlockSpec((virs, 1), lambda t, place: (0, 0)),
        pl.BlockSpec((depth, width), lambda t, place: (0, 0)),
        pl.BlockSpec((depth, width), lambda t, place: (0, 0)),
    ]
    operands = []
    for spans, exact, received, offset, lowest in sums:
        shift = begin - lowest // tile
        spec = pl.BlockSpec(
            (1, exact.shape[1], tile),
            functools.partial(lambda offset, shift, t, place: (offset, 0, shift + t), offset, shift),
        )
        in_specs += [spec, spec]
        operands += [exact, received]
    aliases = {}
    if previous is not None:
        in_specs.append(pl.BlockSpec(memory_space=pl.ANY))
        operands.append(previous)
        aliases = {6 + len(operands) - 1: 0}
    in_specs += [pl.BlockSpec(memory_space=pl.ANY)] * len(after)
    operands += after
    return pl.pallas_call(
        functools.partial(gamma_kernel, [spans for spans, *_ in sums], orbital, parts),
        grid_spec=pltpu.PrefetchScalarGridSpec(
            num_scalar_prefetch=1,
            grid=((right - left) // tile,),
            in_specs=in_specs,
            out_specs=[
                pl.BlockSpec((1, depth, tile), lambda t, place: (place[OWN] + orbital, 0, begin + t)),
            ] + [pl.BlockSpec((depth // parts, tile), lambda t, place: (0, t))] * parts,
            scratch_shapes=[pltpu.VMEM((width, tile), jnp.bfloat16)],
        ),
        out_shape=[
            jax.ShapeDtypeStruct(whole.shape, whole.dtype),
        ] + [jax.ShapeDtypeStruct((depth // parts, right - left), whole.dtype)] * parts,
        input_output_aliases=aliases,
        compiler_params=params(),
        cost_estimate=BRIEF,
    )(place, energies, row, column, near, far, *operands)


def shards(orbital_b, occ_energy, vir_energy):
    occ_index = lax.axis_index("occ")
    aux_index = lax.axis_index("aux")
    occ_count = lax.axis_size("occ")
    aux_count = lax.axis_size("aux")
    chips = aux_count // 2
    rows, depth, virs = orbital_b.shape
    half = rows // 2
    core = aux_index % 2

    def to_mate(value):
        return lax.ppermute(value, "aux", [(at, at ^ 1) for at in range(aux_count)])

    def to_chip(value):
        return lax.ppermute(value, "aux", [(at, (at + 2) % aux_count) for at in range(aux_count)])

    place = jnp.stack([
        core * half,
        occ_index * rows + core * half,
        jnp.maximum(occ_index - 1, 0) * rows,
        jnp.minimum(occ_index + 1, occ_count - 1) * rows,
    ]).astype(jnp.int32)

    unit = virs // 3
    spans = [(partner, start, start + unit) for partner in (0, 1) for start in range(0, virs, unit)]
    groups = [(0, half // 2), (half // 2, half - half // 2)]

    near, far = [], []

    def bring(after):
        partner, start, stop = spans[len(near)]
        columns = orbital_b[0, :, start:stop] if after is None else leader_columns(orbital_b, start, stop, after)
        near.append(shifted(columns, "occ", 1 - 2 * partner))
        far.append(to_mate(near[-1]))
        return columns

    bring(None)
    fetched = to_mate(orbital_b)

    steps = [((piece,), *group, 0, virs) for piece in range(4) for group in groups]
    steps += [((4, 5), at, 1, 0, virs) for at in range(half)]
    brings = {0: 1, 2: 1, 4: 1, 5: 1, 6: 1}
    ahead = 2 if chips == 2 else 1
    arrived, sent, turned, found = [], [], {}, [[] for _ in range(half)]
    rounded = vir_energy
    for at, (pieces, first, count, left, right) in enumerate(steps):
        for piece in pieces:
            if piece not in turned:
                turned[piece] = near[piece].T, far[piece].T
        lead = ahead + (at >= 9) + (at >= 11) if chips == 2 else ahead
        after = [arrived[at - lead] if at >= lead else vir_energy, rounded]
        exact, rounded = partial_integrals(
            place, [turned[piece] for piece in pieces], orbital_b, fetched, first, count, left, right, after
        )
        received = to_chip(rounded) if chips > 1 else jnp.zeros_like(rounded)
        for _ in range(chips - 2):
            exact = exact + received.astype(jnp.float32)
            received = to_chip(received)
        arrived.append(received if chips <= 2 else exact)
        sent.append(rounded)
        for _ in range(brings.get(at, 0)):
            bring(rounded if at else None)
        for offset in range(count):
            found[first + offset].append(([spans[piece] for piece in pieces], exact, received, offset, left))

    leaders = [jnp.concatenate(side, axis=1) for side in (near, far)]
    row, column = vir_energy[None, :], vir_energy[:, None]
    out, owed = None, []
    for orbital in range(half):
        ends = [(0, virs)]
        for left, right in ends:
            sums = found[orbital][:4] + [entry for entry in found[orbital][4:] if entry[-1] == left]
            out, *others = gamma_rows(
                place, occ_energy, row, column, *leaders, orbital, left, right, sums, orbital_b, out, sent[-1:] if orbital == 0 else [],
            )
            owed.append(([to_mate(other) for other in others], orbital, left))
            if len(owed) > 1:
                out = put(out, *owed.pop(0), (1 - core) * half)
    return put(out, *owed.pop(0), (1 - core) * half)


def put(out, parts, orbital, left, offset):
    zero = jnp.zeros((), jnp.int32)
    for part, value in enumerate(parts):
        out = lax.dynamic_update_slice(out, value[None], (offset + orbital, zero + part * value.shape[0], zero + left))
    return out


def solution(mesh):
    placed = (P("occ", "aux", None), P(), P())
    return jax.shard_map(
        shards, mesh=mesh, in_specs=placed, out_specs=P("occ", "aux", None), check_vma=False
    )
```

```python
import functools

import jax
import jax.numpy as jnp
from jax import lax
from jax.experimental import pallas as pl
from jax.experimental.pallas import tpu as pltpu
from jax.sharding import PartitionSpec as P

VMEM_BYTES = 56 * 1024 * 1024

BRIEF = pl.CostEstimate(flops=0, bytes_accessed=0, transcendentals=0)

OWN, OWN_ENERGY, PARTNER_ENERGY = 0, 1, 2


def shifted(value, axis, steps):
    count = lax.axis_size(axis)
    initial, last = (max(0, -steps), min(count, count - steps))
    return lax.ppermute(value, axis, [(source, source + steps) for source in range(initial, last)])


def params():
    return pltpu.CompilerParams(vmem_limit_bytes=VMEM_BYTES)


def columns_kernel(source, after, out):
    out[...] = source[0]


def leader_columns(orbital_b, start, stop, after):
    depth = orbital_b.shape[1]
    width = 128 if (start % 128 == 0 and stop % 128 == 0) else stop - start
    return pl.pallas_call(
        columns_kernel,
        grid=((stop - start) // width,),
        in_specs=[
            pl.BlockSpec((1, depth, width), lambda t: (0, 0, start // width + t)),
            pl.BlockSpec(memory_space=pl.ANY),
        ],
        out_specs=pl.BlockSpec((depth, width), lambda t: (0, t)),
        out_shape=jax.ShapeDtypeStruct((depth, stop - start), orbital_b.dtype),
        compiler_params=params(),
        cost_estimate=BRIEF,
    )(orbital_b, after)


def partial_kernel(pieces, place, *refs):
    near_b, far_b = refs[2 * pieces : 2 * pieces + 2]
    exact, rounded = refs[-2:]
    at = 0
    for piece in range(pieces):
        near, far = refs[2 * piece : 2 * piece + 2]
        total = jnp.dot(near[...], near_b[0], preferred_element_type=jnp.float32)
        total += jnp.dot(far[...], far_b[0], preferred_element_type=jnp.float32)
        here = slice(at, at + near.shape[0])
        exact[0, here] = total
        rounded[0, here] = total.astype(jnp.bfloat16)
        at += near.shape[0]


def partial_integrals(place, leaders, orbital_b, fetched, first, count, left, right, after):
    depth, virs = orbital_b.shape[1:]
    width = sum(near.shape[0] for near, _ in leaders)
    tile = right - left if (right - left) == virs or left % 128 else virs // 3
    begin = left // tile
    own = pl.BlockSpec((1, depth, tile), lambda i, t, place: (place[OWN] + first + i, 0, begin + t))
    grid_spec = pltpu.PrefetchScalarGridSpec(
        num_scalar_prefetch=1,
        grid=(count, (right - left) // tile),
        in_specs=[pl.BlockSpec(side.shape, lambda i, t, place: (0, 0)) for pair in leaders for side in pair]
        + [own, own] + [pl.BlockSpec(memory_space=pl.ANY)] * len(after),
        out_specs=[pl.BlockSpec((1, width, tile), lambda i, t, place: (i, 0, t))] * 2,
    )
    return pl.pallas_call(
        functools.partial(partial_kernel, len(leaders)),
        grid_spec=grid_spec,
        out_shape=[
            jax.ShapeDtypeStruct((count, width, right - left), jnp.float32),
            jax.ShapeDtypeStruct((count, width, right - left), jnp.bfloat16),
        ],
        compiler_params=params(),
        cost_estimate=BRIEF,
    )(place, *[side for pair in leaders for side in pair], orbital_b, fetched, *after)


def gamma_kernel(spans, orbital, parts, place, energies, row, column, near, far, *refs):
    own, outs, amplitude = refs[-2 - parts], refs[-1 - parts : -1], refs[-1]
    own_energy = energies[place[OWN_ENERGY] + orbital]
    at = 0
    for index, ranges in enumerate(spans):
        exact, received = refs[2 * index], refs[2 * index + 1]
        lowest = 0
        for partner, start, stop in ranges:
            here = slice(lowest, lowest + stop - start)
            denominator = (row[...] + column[start:stop]) - own_energy - energies[place[PARTNER_ENERGY + partner]]
            integral = exact[0, here] + received[0, here].astype(jnp.float32)
            amplitude[at : at + stop - start] = (integral / denominator).astype(jnp.bfloat16)
            lowest += stop - start
            at += stop - start
    own[0] = jnp.dot(near[...], amplitude[...], preferred_element_type=jnp.float32).astype(own.dtype)
    other = jnp.dot(far[...], amplitude[...], preferred_element_type=jnp.float32).astype(own.dtype)
    rows = other.shape[0] // parts
    for part, out in enumerate(outs):
        out[...] = other[part * rows : (part + 1) * rows]


def gamma_rows(place, energies, row, column, near, far, orbital, left, right, sums, whole, previous, after):
    depth, width = near.shape
    virs = row.shape[1]
    tile = virs // 3
    begin = left // tile
    parts = next(count for count in (3, 2, 1) if depth % (16 * count) == 0 or count == 1)
    in_specs = [
        pl.BlockSpec(memory_space=pltpu.SMEM),
        pl.BlockSpec((1, tile), lambda t, place: (0, begin + t)),
        pl.BlockSpec((virs, 1), lambda t, place: (0, 0)),
        pl.BlockSpec((depth, width), lambda t, place: (0, 0)),
        pl.BlockSpec((depth, width), lambda t, place: (0, 0)),
    ]
    operands = []
    for spans, exact, received, offset, lowest in sums:
        shift = begin - lowest // tile
        spec = pl.BlockSpec(
            (1, exact.shape[1], tile),
            functools.partial(lambda offset, shift, t, place: (offset, 0, shift + t), offset, shift),
        )
        in_specs += [spec, spec]
        operands += [exact, received]
    aliases = {}
    if previous is not None:
        in_specs.append(pl.BlockSpec(memory_space=pl.ANY))
        operands.append(previous)
        aliases = {6 + len(operands) - 1: 0}
    in_specs += [pl.BlockSpec(memory_space=pl.ANY)] * len(after)
    operands += after
    return pl.pallas_call(
        functools.partial(gamma_kernel, [spans for spans, *_ in sums], orbital, parts),
        grid_spec=pltpu.PrefetchScalarGridSpec(
            num_scalar_prefetch=1,
            grid=((right - left) // tile,),
            in_specs=in_specs,
            out_specs=[
                pl.BlockSpec((1, depth, tile), lambda t, place: (place[OWN] + orbital, 0, begin + t)),
            ] + [pl.BlockSpec((depth // parts, tile), lambda t, place: (0, t))] * parts,
            scratch_shapes=[pltpu.VMEM((width, tile), jnp.bfloat16)],
        ),
        out_shape=[
            jax.ShapeDtypeStruct(whole.shape, whole.dtype),
        ] + [jax.ShapeDtypeStruct((depth // parts, right - left), whole.dtype)] * parts,
        input_output_aliases=aliases,
        compiler_params=params(),
        cost_estimate=BRIEF,
    )(place, energies, row, column, near, far, *operands)


def shards(orbital_b, occ_energy, vir_energy):
    occ_index = lax.axis_index("occ")
    aux_index = lax.axis_index("aux")
    occ_count = lax.axis_size("occ")
    aux_count = lax.axis_size("aux")
    chips = aux_count // 2
    rows, depth, virs = orbital_b.shape
    half = rows // 2
    core = aux_index % 2

    def to_mate(value):
        return lax.ppermute(value, "aux", [(at, at ^ 1) for at in range(aux_count)])

    def to_chip(value):
        return lax.ppermute(value, "aux", [(at, (at + 2) % aux_count) for at in range(aux_count)])

    place = jnp.stack([
        core * half,
        occ_index * rows + core * half,
        jnp.maximum(occ_index - 1, 0) * rows,
        jnp.minimum(occ_index + 1, occ_count - 1) * rows,
    ]).astype(jnp.int32)

    unit = virs // 3
    spans = [(partner, start, start + unit) for partner in (0, 1) for start in range(0, virs, unit)]
    groups = [(0, half // 2), (half // 2, half - half // 2)]

    near, far = [], []

    def bring(after):
        partner, start, stop = spans[len(near)]
        columns = orbital_b[0, :, start:stop] if after is None else leader_columns(orbital_b, start, stop, after)
        near.append(shifted(columns, "occ", 1 - 2 * partner))
        far.append(to_mate(near[-1]))
        return columns

    bring(None)
    fetched = to_mate(orbital_b)

    steps = [((piece,), *group, 0, virs) for piece in range(3) for group in groups]
    steps += [((3, 4, 5), at, 1, 0, virs) for at in range(half)]
    brings = {0: 1, 2: 1, 3: 2, 4: 1}
    ahead = 2 if chips == 2 else 1
    arrived, sent, turned, found = [], [], {}, [[] for _ in range(half)]
    rounded = vir_energy
    for at, (pieces, first, count, left, right) in enumerate(steps):
        for piece in pieces:
            if piece not in turned:
                turned[piece] = near[piece].T, far[piece].T
        lead = ahead + (at >= 8) + (at >= 9) if chips == 2 else ahead
        after = [arrived[at - lead] if at >= lead else vir_energy, rounded]
        exact, rounded = partial_integrals(
            place, [turned[piece] for piece in pieces], orbital_b, fetched, first, count, left, right, after
        )
        received = to_chip(rounded) if chips > 1 else jnp.zeros_like(rounded)
        for _ in range(chips - 2):
            exact = exact + received.astype(jnp.float32)
            received = to_chip(received)
        arrived.append(received if chips <= 2 else exact)
        sent.append(rounded)
        for _ in range(brings.get(at, 0)):
            bring(rounded if at else None)
        for offset in range(count):
            found[first + offset].append(([spans[piece] for piece in pieces], exact, received, offset, left))

    leaders = [jnp.concatenate(side, axis=1) for side in (near, far)]
    row, column = vir_energy[None, :], vir_energy[:, None]
    out, owed = None, []
    for orbital in range(half):
        ends = [(0, virs)]
        for left, right in ends:
            sums = found[orbital]
            out, *others = gamma_rows(
                place, occ_energy, row, column, *leaders, orbital, left, right, sums, orbital_b, out, sent[-1:] if orbital == 0 else [],
            )
            owed.append(([to_mate(other) for other in others], orbital, left))
            if len(owed) > 1:
                out = put(out, *owed.pop(0), (1 - core) * half)
    return put(out, *owed.pop(0), (1 - core) * half)


def put(out, parts, orbital, left, offset):
    zero = jnp.zeros((), jnp.int32)
    for part, value in enumerate(parts):
        out = lax.dynamic_update_slice(out, value[None], (offset + orbital, zero + part * value.shape[0], zero + left))
    return out


def solution(mesh):
    placed = (P("occ", "aux", None), P(), P())
    return jax.shard_map(
        shards, mesh=mesh, in_specs=placed, out_specs=P("occ", "aux", None), check_vma=False
    )
```

```python
import functools

import jax
import jax.numpy as jnp
from jax import lax
from jax.experimental import pallas as pl
from jax.experimental.pallas import tpu as pltpu
from jax.sharding import PartitionSpec as P

VMEM_BYTES = 56 * 1024 * 1024

BRIEF = pl.CostEstimate(flops=0, bytes_accessed=0, transcendentals=0)

OWN, OWN_ENERGY, PARTNER_ENERGY = 0, 1, 2


def shifted(value, axis, steps):
    count = lax.axis_size(axis)
    initial, last = (max(0, -steps), min(count, count - steps))
    return lax.ppermute(value, axis, [(source, source + steps) for source in range(initial, last)])


def params():
    return pltpu.CompilerParams(vmem_limit_bytes=VMEM_BYTES)


def columns_kernel(source, after, out):
    out[...] = source[0]


def leader_columns(orbital_b, start, stop, after):
    depth = orbital_b.shape[1]
    width = 128 if (start % 128 == 0 and stop % 128 == 0) else stop - start
    return pl.pallas_call(
        columns_kernel,
        grid=((stop - start) // width,),
        in_specs=[
            pl.BlockSpec((1, depth, width), lambda t: (0, 0, start // width + t)),
            pl.BlockSpec(memory_space=pl.ANY),
        ],
        out_specs=pl.BlockSpec((depth, width), lambda t: (0, t)),
        out_shape=jax.ShapeDtypeStruct((depth, stop - start), orbital_b.dtype),
        compiler_params=params(),
        cost_estimate=BRIEF,
    )(orbital_b, after)


def partial_kernel(pieces, place, *refs):
    near_b, far_b = refs[2 * pieces : 2 * pieces + 2]
    exact, rounded = refs[-2:]
    at = 0
    for piece in range(pieces):
        near, far = refs[2 * piece : 2 * piece + 2]
        total = jnp.dot(near[...], near_b[0], preferred_element_type=jnp.float32)
        total += jnp.dot(far[...], far_b[0], preferred_element_type=jnp.float32)
        here = slice(at, at + near.shape[0])
        exact[0, here] = total
        rounded[0, here] = total.astype(jnp.bfloat16)
        at += near.shape[0]


def partial_integrals(place, leaders, orbital_b, fetched, first, count, left, right, after):
    depth, virs = orbital_b.shape[1:]
    width = sum(near.shape[0] for near, _ in leaders)
    tile = right - left if (right - left) == virs or left % 128 else virs // 3
    begin = left // tile
    own = pl.BlockSpec((1, depth, tile), lambda i, t, place: (place[OWN] + first + i, 0, begin + t))
    grid_spec = pltpu.PrefetchScalarGridSpec(
        num_scalar_prefetch=1,
        grid=(count, (right - left) // tile),
        in_specs=[pl.BlockSpec(side.shape, lambda i, t, place: (0, 0)) for pair in leaders for side in pair]
        + [own, own] + [pl.BlockSpec(memory_space=pl.ANY)] * len(after),
        out_specs=[pl.BlockSpec((1, width, tile), lambda i, t, place: (i, 0, t))] * 2,
    )
    return pl.pallas_call(
        functools.partial(partial_kernel, len(leaders)),
        grid_spec=grid_spec,
        out_shape=[
            jax.ShapeDtypeStruct((count, width, right - left), jnp.float32),
            jax.ShapeDtypeStruct((count, width, right - left), jnp.bfloat16),
        ],
        compiler_params=params(),
        cost_estimate=BRIEF,
    )(place, *[side for pair in leaders for side in pair], orbital_b, fetched, *after)


def gamma_kernel(spans, orbital, given, parts, place, energies, row, column, near, far, *refs):
    own, outs, amplitude = refs[-2 - parts], refs[-1 - parts : -1], refs[-1]
    own_energy = energies[place[OWN_ENERGY] + orbital]
    at = 0
    for index, ranges in enumerate(spans):
        exact, received = refs[2 * index], refs[2 * index + 1]
        lowest = 0
        for partner, start, stop in ranges:
            here = slice(lowest, lowest + stop - start)
            denominator = (row[...] + column[start:stop]) - own_energy - energies[place[PARTNER_ENERGY + partner]]
            other = received[0, here].astype(jnp.float32)
            value = (exact[0, here] + other) / denominator
            if index == given:
                value = jnp.where(place[OWN] == 0, other, value)
            amplitude[at : at + stop - start] = value.astype(jnp.bfloat16)
            lowest += stop - start
            at += stop - start
    own[0] = jnp.dot(near[...], amplitude[...], preferred_element_type=jnp.float32).astype(own.dtype)
    other = jnp.dot(far[...], amplitude[...], preferred_element_type=jnp.float32).astype(own.dtype)
    rows = other.shape[0] // parts
    for part, out in enumerate(outs):
        out[...] = other[part * rows : (part + 1) * rows]


def gamma_rows(place, energies, row, column, near, far, orbital, left, right, sums, given, whole, previous, after):
    depth, width = near.shape
    virs = row.shape[1]
    tile = virs // 3
    begin = left // tile
    parts = next(count for count in (3, 2, 1) if depth % (16 * count) == 0 or count == 1)
    in_specs = [
        pl.BlockSpec(memory_space=pltpu.SMEM),
        pl.BlockSpec((1, tile), lambda t, place: (0, begin + t)),
        pl.BlockSpec((virs, 1), lambda t, place: (0, 0)),
        pl.BlockSpec((depth, width), lambda t, place: (0, 0)),
        pl.BlockSpec((depth, width), lambda t, place: (0, 0)),
    ]
    operands = []
    for spans, exact, received, offset, lowest in sums:
        shift = begin - lowest // tile
        spec = pl.BlockSpec(
            (1, exact.shape[1], tile),
            functools.partial(lambda offset, shift, t, place: (offset, 0, shift + t), offset, shift),
        )
        in_specs += [spec, spec]
        operands += [exact, received]
    aliases = {}
    if previous is not None:
        in_specs.append(pl.BlockSpec(memory_space=pl.ANY))
        operands.append(previous)
        aliases = {6 + len(operands) - 1: 0}
    in_specs += [pl.BlockSpec(memory_space=pl.ANY)] * len(after)
    operands += after
    return pl.pallas_call(
        functools.partial(gamma_kernel, [spans for spans, *_ in sums], orbital, given, parts),
        grid_spec=pltpu.PrefetchScalarGridSpec(
            num_scalar_prefetch=1,
            grid=((right - left) // tile,),
            in_specs=in_specs,
            out_specs=[
                pl.BlockSpec((1, depth, tile), lambda t, place: (place[OWN] + orbital, 0, begin + t)),
            ] + [pl.BlockSpec((depth // parts, tile), lambda t, place: (0, t))] * parts,
            scratch_shapes=[pltpu.VMEM((width, tile), jnp.bfloat16)],
        ),
        out_shape=[
            jax.ShapeDtypeStruct(whole.shape, whole.dtype),
        ] + [jax.ShapeDtypeStruct((depth // parts, right - left), whole.dtype)] * parts,
        input_output_aliases=aliases,
        compiler_params=params(),
        cost_estimate=BRIEF,
    )(place, energies, row, column, near, far, *operands)


def turned_kernel(spans, place, energies, row, column, *refs):
    sums, out = refs[:-1], refs[-1]
    for index, (partner, start, stop) in enumerate(spans):
        denominator = (row[...] + column[start:stop]) - energies[place[OWN_ENERGY]] - energies[place[PARTNER_ENERGY + partner]]
        integral = sums[2 * index][0] + sums[2 * index + 1][0].astype(jnp.float32)
        out[:, start:stop] = (integral / denominator).T.astype(jnp.bfloat16)


def turned_amplitudes(place, energies, row, column, sums):
    virs = row.shape[1]
    tile = virs // 3
    in_specs = [
        pl.BlockSpec(memory_space=pltpu.SMEM),
        pl.BlockSpec((1, tile), lambda t, place: (0, t)),
        pl.BlockSpec((virs, 1), lambda t, place: (0, 0)),
    ]
    operands = []
    for _, exact, received, offset, _ in sums:
        spec = pl.BlockSpec((1, exact.shape[1], tile), functools.partial(lambda offset, t, place: (offset, 0, t), offset))
        in_specs += [spec, spec]
        operands += [exact, received]
    return pl.pallas_call(
        functools.partial(turned_kernel, [span for spans, *_ in sums for span in spans]),
        grid_spec=pltpu.PrefetchScalarGridSpec(
            num_scalar_prefetch=1,
            grid=(virs // tile,),
            in_specs=in_specs,
            out_specs=pl.BlockSpec((tile, virs), lambda t, place: (t, 0)),
        ),
        out_shape=jax.ShapeDtypeStruct((virs, virs), jnp.bfloat16),
        compiler_params=params(),
        cost_estimate=BRIEF,
    )(place, energies, row, column, *operands)


def shards(orbital_b, occ_energy, vir_energy):
    occ_index = lax.axis_index("occ")
    aux_index = lax.axis_index("aux")
    occ_count = lax.axis_size("occ")
    aux_count = lax.axis_size("aux")
    chips = aux_count // 2
    rows, depth, virs = orbital_b.shape
    half = rows // 2
    core = aux_index % 2

    def to_mate(value):
        return lax.ppermute(value, "aux", [(at, at ^ 1) for at in range(aux_count)])

    def to_chip(value):
        return lax.ppermute(value, "aux", [(at, (at + 2) % aux_count) for at in range(aux_count)])

    def leader_swap(value):
        pairs = []
        for block in range(occ_count):
            for at in range(aux_count):
                if at % 2:
                    pairs.append((block * aux_count + at, block * aux_count + (at + 2) % aux_count))
                elif block:
                    pairs.append((block * aux_count + at, (block - 1) * aux_count + at))
        return lax.ppermute(value, ("occ", "aux"), pairs)

    place = jnp.stack([
        core * half,
        occ_index * rows + core * half,
        jnp.maximum(occ_index - 1, 0) * rows,
        jnp.minimum(occ_index + 1, occ_count - 1) * rows,
    ]).astype(jnp.int32)

    unit = virs // 3
    spans = [(partner, start, start + unit) for partner in (0, 1) for start in range(0, virs, unit)]
    groups = [(0, half // 2), (half // 2, half - half // 2)]

    near, far = [], []

    def bring(after):
        partner, start, stop = spans[len(near)]
        columns = orbital_b[0, :, start:stop] if after is None else leader_columns(orbital_b, start, stop, after)
        near.append(shifted(columns, "occ", 1 - 2 * partner))
        far.append(to_mate(near[-1]))
        return columns

    bring(None)
    fetched = to_mate(orbital_b)

    steps = [((piece,), *group, 0, virs) for piece in range(3) for group in groups]
    order = [1, 0, *range(2, half)] if half > 2 else list(range(half))
    steps += [((3, 4, 5), at, 1, 0, virs) for at in order]
    brings = {0: 1, 2: 1, 3: 2, 4: 1}
    ahead = 2 if chips == 2 else 1
    row, column = vir_energy[None, :], vir_energy[:, None]
    arrived, sent, turned, found = [], [], {}, [[] for _ in range(half)]
    rounded = vir_energy
    for at, (pieces, first, count, left, right) in enumerate(steps):
        for piece in pieces:
            if piece not in turned:
                turned[piece] = near[piece].T, far[piece].T
        lead = ahead + (at >= 8) + (at >= 9) if chips == 2 else ahead
        after = [arrived[at - lead] if at >= lead else vir_energy, rounded]
        exact, rounded = partial_integrals(
            place, [turned[piece] for piece in pieces], orbital_b, fetched, first, count, left, right, after
        )
        if len(pieces) > 1 and first == 0 and chips == 2:
            turned_leader = turned_amplitudes(place, occ_energy, row, column, found[0])
            received = leader_swap(jnp.where(core == 0, turned_leader[None], rounded))
        else:
            received = to_chip(rounded) if chips > 1 else jnp.zeros_like(rounded)
        for _ in range(chips - 2):
            exact = exact + received.astype(jnp.float32)
            received = to_chip(received)
        arrived.append(received if chips <= 2 else exact)
        sent.append(rounded)
        for _ in range(brings.get(at, 0)):
            bring(rounded if at else None)
        for offset in range(count):
            found[first + offset].append(([spans[piece] for piece in pieces], exact, received, offset, left))

    leaders = [jnp.concatenate(side, axis=1) for side in (near, far)]
    out, owed = None, []
    for orbital in order:
        while len(owed) > (1 if orbital != order[-1] else 0):
            out = put(out, *owed.pop(0), (1 - core) * half)
        out, *others = gamma_rows(
            place, occ_energy, row, column, *leaders, orbital, 0, virs, found[orbital],
            len(found[orbital]) - 1 if orbital == 0 and chips == 2 else None, orbital_b, out, sent[-1:] if out is None else [],
        )
        owed.append(([to_mate(other) for other in others], orbital, 0))
    while owed:
        out = put(out, *owed.pop(0), (1 - core) * half)
    return out


def put(out, parts, orbital, left, offset):
    zero = jnp.zeros((), jnp.int32)
    for part, value in enumerate(parts):
        out = lax.dynamic_update_slice(out, value[None], (offset + orbital, zero + part * value.shape[0], zero + left))
    return out


def solution(mesh):
    placed = (P("occ", "aux", None), P(), P())
    return jax.shard_map(
        shards, mesh=mesh, in_specs=placed, out_specs=P("occ", "aux", None), check_vma=False
    )
```

```python
import functools

import jax
import jax.numpy as jnp
from jax import lax
from jax.experimental import pallas as pl
from jax.experimental.pallas import tpu as pltpu
from jax.sharding import PartitionSpec as P

VMEM_BYTES = 56 * 1024 * 1024
GAMMA_BYTES = 40 * 1024 * 1024

BRIEF = pl.CostEstimate(flops=0, bytes_accessed=0, transcendentals=0)

OWN, OWN_ENERGY, PARTNER_ENERGY = 0, 1, 2


def shifted(value, axis, steps):
    count = lax.axis_size(axis)
    initial, last = (max(0, -steps), min(count, count - steps))
    return lax.ppermute(value, axis, [(source, source + steps) for source in range(initial, last)])


def params(limit=VMEM_BYTES):
    return pltpu.CompilerParams(vmem_limit_bytes=limit)


def columns_kernel(source, after, out):
    out[...] = source[0]


def leader_columns(orbital_b, start, stop, after):
    depth = orbital_b.shape[1]
    width = 128 if (start % 128 == 0 and stop % 128 == 0) else stop - start
    return pl.pallas_call(
        columns_kernel,
        grid=((stop - start) // width,),
        in_specs=[
            pl.BlockSpec((1, depth, width), lambda t: (0, 0, start // width + t)),
            pl.BlockSpec(memory_space=pl.ANY),
        ],
        out_specs=pl.BlockSpec((depth, width), lambda t: (0, t)),
        out_shape=jax.ShapeDtypeStruct((depth, stop - start), orbital_b.dtype),
        compiler_params=params(),
        cost_estimate=BRIEF,
    )(orbital_b, after)


def partial_kernel(pieces, place, *refs):
    near_b, far_b = refs[2 * pieces : 2 * pieces + 2]
    exact, rounded = refs[-2:]
    at = 0
    for piece in range(pieces):
        near, far = refs[2 * piece : 2 * piece + 2]
        total = jnp.dot(near[...], near_b[0], preferred_element_type=jnp.float32)
        total += jnp.dot(far[...], far_b[0], preferred_element_type=jnp.float32)
        here = slice(at, at + near.shape[0])
        exact[0, here] = total
        rounded[0, here] = total.astype(jnp.bfloat16)
        at += near.shape[0]


def partial_integrals(place, leaders, orbital_b, fetched, first, count, left, right, after):
    depth, virs = orbital_b.shape[1:]
    width = sum(near.shape[0] for near, _ in leaders)
    tile = right - left if (right - left) == virs or left % 128 else virs // 3
    begin = left // tile
    own = pl.BlockSpec((1, depth, tile), lambda i, t, place: (place[OWN] + first + i, 0, begin + t))
    grid_spec = pltpu.PrefetchScalarGridSpec(
        num_scalar_prefetch=1,
        grid=(count, (right - left) // tile),
        in_specs=[pl.BlockSpec(side.shape, lambda i, t, place: (0, 0)) for pair in leaders for side in pair]
        + [own, own] + [pl.BlockSpec(memory_space=pl.ANY)] * len(after),
        out_specs=[pl.BlockSpec((1, width, tile), lambda i, t, place: (i, 0, t))] * 2,
    )
    return pl.pallas_call(
        functools.partial(partial_kernel, len(leaders)),
        grid_spec=grid_spec,
        out_shape=[
            jax.ShapeDtypeStruct((count, width, right - left), jnp.float32),
            jax.ShapeDtypeStruct((count, width, right - left), jnp.bfloat16),
        ],
        compiler_params=params(),
        cost_estimate=BRIEF,
    )(place, *[side for pair in leaders for side in pair], orbital_b, fetched, *after)


def gamma_kernel(spans, orbital, given, parts, place, energies, row, column, near, far, *refs):
    own, outs, amplitude = refs[-2 - parts], refs[-1 - parts : -1], refs[-1]
    own_energy = energies[place[OWN_ENERGY] + orbital]
    at = 0
    for index, ranges in enumerate(spans):
        exact, received = refs[2 * index], refs[2 * index + 1]
        lowest = 0
        for partner, start, stop in ranges:
            here = slice(lowest, lowest + stop - start)
            denominator = (row[...] + column[start:stop]) - own_energy - energies[place[PARTNER_ENERGY + partner]]
            other = received[0, here].astype(jnp.float32)
            value = (exact[0, here] + other) / denominator
            if index == given:
                value = jnp.where(place[OWN] == 0, other, value)
            amplitude[at : at + stop - start] = value.astype(jnp.bfloat16)
            lowest += stop - start
            at += stop - start
    own[0] = jnp.dot(near[...], amplitude[...], preferred_element_type=jnp.float32).astype(own.dtype)
    other = jnp.dot(far[...], amplitude[...], preferred_element_type=jnp.float32).astype(own.dtype)
    rows = other.shape[0] // parts
    for part, out in enumerate(outs):
        out[...] = other[part * rows : (part + 1) * rows]


def gamma_rows(place, energies, row, column, near, far, orbital, left, right, sums, given, whole, previous, after, parts):
    depth, width = near.shape
    virs = row.shape[1]
    tile = virs // 3
    begin = left // tile
    in_specs = [
        pl.BlockSpec(memory_space=pltpu.SMEM),
        pl.BlockSpec((1, tile), lambda t, place: (0, begin + t)),
        pl.BlockSpec((virs, 1), lambda t, place: (0, 0)),
        pl.BlockSpec((depth, width), lambda t, place: (0, 0)),
        pl.BlockSpec((depth, width), lambda t, place: (0, 0)),
    ]
    operands = []
    for spans, exact, received, offset, lowest in sums:
        shift = begin - lowest // tile
        spec = pl.BlockSpec(
            (1, exact.shape[1], tile),
            functools.partial(lambda offset, shift, t, place: (offset, 0, shift + t), offset, shift),
        )
        in_specs += [spec, spec]
        operands += [exact, received]
    aliases = {}
    if previous is not None:
        in_specs.append(pl.BlockSpec(memory_space=pl.ANY))
        operands.append(previous)
        aliases = {6 + len(operands) - 1: 0}
    in_specs += [pl.BlockSpec(memory_space=pl.ANY)] * len(after)
    operands += after
    return pl.pallas_call(
        functools.partial(gamma_kernel, [spans for spans, *_ in sums], orbital, given, parts),
        grid_spec=pltpu.PrefetchScalarGridSpec(
            num_scalar_prefetch=1,
            grid=((right - left) // tile,),
            in_specs=in_specs,
            out_specs=[
                pl.BlockSpec((1, depth, tile), lambda t, place: (place[OWN] + orbital, 0, begin + t)),
            ] + [pl.BlockSpec((depth // parts, tile), lambda t, place: (0, t))] * parts,
            scratch_shapes=[pltpu.VMEM((width, tile), jnp.bfloat16)],
        ),
        out_shape=[
            jax.ShapeDtypeStruct(whole.shape, whole.dtype),
        ] + [jax.ShapeDtypeStruct((depth // parts, right - left), whole.dtype)] * parts,
        input_output_aliases=aliases,
        compiler_params=params(GAMMA_BYTES),
        cost_estimate=BRIEF,
    )(place, energies, row, column, near, far, *operands)


def turned_kernel(spans, place, energies, row, column, *refs):
    sums, out = refs[:-1], refs[-1]
    for index, (partner, start, stop) in enumerate(spans):
        denominator = (row[...] + column[start:stop]) - energies[place[OWN_ENERGY]] - energies[place[PARTNER_ENERGY + partner]]
        integral = sums[2 * index][0] + sums[2 * index + 1][0].astype(jnp.float32)
        out[:, start:stop] = (integral / denominator).T.astype(jnp.bfloat16)


def turned_amplitudes(place, energies, row, column, sums):
    virs = row.shape[1]
    tile = virs // 3
    in_specs = [
        pl.BlockSpec(memory_space=pltpu.SMEM),
        pl.BlockSpec((1, tile), lambda t, place: (0, t)),
        pl.BlockSpec((virs, 1), lambda t, place: (0, 0)),
    ]
    operands = []
    for _, exact, received, offset, _ in sums:
        spec = pl.BlockSpec((1, exact.shape[1], tile), functools.partial(lambda offset, t, place: (offset, 0, t), offset))
        in_specs += [spec, spec]
        operands += [exact, received]
    return pl.pallas_call(
        functools.partial(turned_kernel, [span for spans, *_ in sums for span in spans]),
        grid_spec=pltpu.PrefetchScalarGridSpec(
            num_scalar_prefetch=1,
            grid=(virs // tile,),
            in_specs=in_specs,
            out_specs=pl.BlockSpec((tile, virs), lambda t, place: (t, 0)),
        ),
        out_shape=jax.ShapeDtypeStruct((virs, virs), jnp.bfloat16),
        compiler_params=params(),
        cost_estimate=BRIEF,
    )(place, energies, row, column, *operands)


def shards(orbital_b, occ_energy, vir_energy):
    occ_index = lax.axis_index("occ")
    aux_index = lax.axis_index("aux")
    occ_count = lax.axis_size("occ")
    aux_count = lax.axis_size("aux")
    chips = aux_count // 2
    rows, depth, virs = orbital_b.shape
    half = rows // 2
    core = aux_index % 2

    def to_mate(value):
        return lax.ppermute(value, "aux", [(at, at ^ 1) for at in range(aux_count)])

    def to_chip(value):
        return lax.ppermute(value, "aux", [(at, (at + 2) % aux_count) for at in range(aux_count)])

    def leader_swap(value):
        pairs = []
        for block in range(occ_count):
            for at in range(aux_count):
                if at % 2:
                    pairs.append((block * aux_count + at, block * aux_count + (at + 2) % aux_count))
                elif block:
                    pairs.append((block * aux_count + at, (block - 1) * aux_count + at))
        return lax.ppermute(value, ("occ", "aux"), pairs)

    place = jnp.stack([
        core * half,
        occ_index * rows + core * half,
        jnp.maximum(occ_index - 1, 0) * rows,
        jnp.minimum(occ_index + 1, occ_count - 1) * rows,
    ]).astype(jnp.int32)

    unit = virs // 3
    spans = [(partner, start, start + unit) for partner in (0, 1) for start in range(0, virs, unit)]
    groups = [(0, half // 2), (half // 2, half - half // 2)]

    near, far = [], []

    def bring(after):
        partner, start, stop = spans[len(near)]
        columns = orbital_b[0, :, start:stop] if after is None else leader_columns(orbital_b, start, stop, after)
        near.append(shifted(columns, "occ", 1 - 2 * partner))
        far.append(to_mate(near[-1]))
        return columns

    bring(None)
    fetched = to_mate(orbital_b)

    steps = [((piece,), *group, 0, virs) for piece in range(3) for group in groups]
    order = [1, 0, *range(2, half)] if half > 2 else list(range(half))
    steps += [((3, 4, 5), at, 1, 0, virs) for at in order]
    brings = {0: 1, 2: 1, 3: 2, 4: 1}
    ahead = 2 if chips == 2 else 1
    row, column = vir_energy[None, :], vir_energy[:, None]
    arrived, sent, turned, found = [], [], {}, [[] for _ in range(half)]
    rounded = vir_energy
    for at, (pieces, first, count, left, right) in enumerate(steps):
        for piece in pieces:
            if piece not in turned:
                turned[piece] = near[piece].T, far[piece].T
        lead = ahead + (at >= 8) + (at >= 9) if chips == 2 else ahead
        after = [arrived[at - lead] if at >= lead else vir_energy, rounded]
        exact, rounded = partial_integrals(
            place, [turned[piece] for piece in pieces], orbital_b, fetched, first, count, left, right, after
        )
        if len(pieces) > 1 and first == 0 and chips == 2:
            turned_leader = turned_amplitudes(place, occ_energy, row, column, found[0])
            received = leader_swap(jnp.where(core == 0, turned_leader[None], rounded))
        else:
            received = to_chip(rounded) if chips > 1 else jnp.zeros_like(rounded)
        for _ in range(chips - 2):
            exact = exact + received.astype(jnp.float32)
            received = to_chip(received)
        arrived.append(received if chips <= 2 else exact)
        sent.append(rounded)
        for _ in range(brings.get(at, 0)):
            bring(rounded if at else None)
        for offset in range(count):
            found[first + offset].append(([spans[piece] for piece in pieces], exact, received, offset, left))

    leaders = [jnp.concatenate(side, axis=1) for side in (near, far)]
    out, owed = None, []
    for orbital in order:
        while len(owed) > (1 if orbital != order[-1] else 0):
            out = put(out, *owed.pop(0), (1 - core) * half)
        out, *others = gamma_rows(
            place, occ_energy, row, column, *leaders, orbital, 0, virs, found[orbital],
            len(found[orbital]) - 1 if orbital == 0 and chips == 2 else None, orbital_b, out, sent[-1:] if out is None else [],
            1 if orbital == order[-1] or depth % 48 else 3,
        )
        owed.append(([to_mate(other) for other in others], orbital, 0))
    while owed:
        out = put(out, *owed.pop(0), (1 - core) * half)
    return out


def put(out, parts, orbital, left, offset):
    zero = jnp.zeros((), jnp.int32)
    for part, value in enumerate(parts):
        out = lax.dynamic_update_slice(out, value[None], (offset + orbital, zero + part * value.shape[0], zero + left))
    return out


def solution(mesh):
    placed = (P("occ", "aux", None), P(), P())
    return jax.shard_map(
        shards, mesh=mesh, in_specs=placed, out_specs=P("occ", "aux", None), check_vma=False
    )
```

```python
import functools

import jax
import jax.numpy as jnp
from jax import lax
from jax.experimental import pallas as pl
from jax.experimental.pallas import tpu as pltpu
from jax.sharding import PartitionSpec as P

VMEM_BYTES = 56 * 1024 * 1024
GAMMA_BYTES = 40 * 1024 * 1024

BRIEF = pl.CostEstimate(flops=0, bytes_accessed=0, transcendentals=0)

OWN, OWN_ENERGY, PARTNER_ENERGY = 0, 1, 2


def shifted(value, axis, steps):
    count = lax.axis_size(axis)
    initial, last = (max(0, -steps), min(count, count - steps))
    return lax.ppermute(value, axis, [(source, source + steps) for source in range(initial, last)])


def params(limit=VMEM_BYTES):
    return pltpu.CompilerParams(vmem_limit_bytes=limit)


def columns_kernel(source, after, out):
    out[...] = source[0]


def leader_columns(orbital_b, start, stop, after):
    depth = orbital_b.shape[1]
    width = 128 if (start % 128 == 0 and stop % 128 == 0) else stop - start
    return pl.pallas_call(
        columns_kernel,
        grid=((stop - start) // width,),
        in_specs=[
            pl.BlockSpec((1, depth, width), lambda t: (0, 0, start // width + t)),
            pl.BlockSpec(memory_space=pl.ANY),
        ],
        out_specs=pl.BlockSpec((depth, width), lambda t: (0, t)),
        out_shape=jax.ShapeDtypeStruct((depth, stop - start), orbital_b.dtype),
        compiler_params=params(),
        cost_estimate=BRIEF,
    )(orbital_b, after)


def partial_kernel(pieces, place, *refs):
    near_b, far_b = refs[2 * pieces : 2 * pieces + 2]
    exact, rounded = refs[-2:]
    at = 0
    for piece in range(pieces):
        near, far = refs[2 * piece : 2 * piece + 2]
        total = jnp.dot(near[...], near_b[0], preferred_element_type=jnp.float32)
        total += jnp.dot(far[...], far_b[0], preferred_element_type=jnp.float32)
        here = slice(at, at + near.shape[0])
        exact[0, here] = total
        rounded[0, here] = total.astype(jnp.bfloat16)
        at += near.shape[0]


def partial_integrals(place, leaders, orbital_b, fetched, first, count, left, right, after):
    depth, virs = orbital_b.shape[1:]
    width = sum(near.shape[0] for near, _ in leaders)
    tile = right - left if (right - left) == virs or left % 128 else virs // 3
    begin = left // tile
    own = pl.BlockSpec((1, depth, tile), lambda i, t, place: (place[OWN] + first + i, 0, begin + t))
    grid_spec = pltpu.PrefetchScalarGridSpec(
        num_scalar_prefetch=1,
        grid=(count, (right - left) // tile),
        in_specs=[pl.BlockSpec(side.shape, lambda i, t, place: (0, 0)) for pair in leaders for side in pair]
        + [own, own] + [pl.BlockSpec(memory_space=pl.ANY)] * len(after),
        out_specs=[pl.BlockSpec((1, width, tile), lambda i, t, place: (i, 0, t))] * 2,
    )
    return pl.pallas_call(
        functools.partial(partial_kernel, len(leaders)),
        grid_spec=grid_spec,
        out_shape=[
            jax.ShapeDtypeStruct((count, width, right - left), jnp.float32),
            jax.ShapeDtypeStruct((count, width, right - left), jnp.bfloat16),
        ],
        compiler_params=params(),
        cost_estimate=BRIEF,
    )(place, *[side for pair in leaders for side in pair], orbital_b, fetched, *after)


def gamma_kernel(spans, orbital, given, parts, place, energies, row, column, near, far, *refs):
    own, outs, amplitude = refs[-2 - parts], refs[-1 - parts : -1], refs[-1]
    own_energy = energies[place[OWN_ENERGY] + orbital]
    at = 0
    for index, ranges in enumerate(spans):
        exact, received = refs[2 * index], refs[2 * index + 1]
        lowest = 0
        for partner, start, stop in ranges:
            here = slice(lowest, lowest + stop - start)
            denominator = (row[...] + column[start:stop]) - own_energy - energies[place[PARTNER_ENERGY + partner]]
            other = received[0, here].astype(jnp.float32)
            value = (exact[0, here] + other) / denominator
            if index == given:
                value = jnp.where(place[OWN] == 0, other, value)
            amplitude[at : at + stop - start] = value.astype(jnp.bfloat16)
            lowest += stop - start
            at += stop - start
    own[0] = jnp.dot(near[...], amplitude[...], preferred_element_type=jnp.float32).astype(own.dtype)
    other = jnp.dot(far[...], amplitude[...], preferred_element_type=jnp.float32).astype(own.dtype)
    rows = other.shape[0] // parts
    for part, out in enumerate(outs):
        out[...] = other[part * rows : (part + 1) * rows]


def gamma_rows(place, energies, row, column, near, far, orbital, left, right, sums, given, whole, previous, after, parts):
    depth, width = near.shape
    virs = row.shape[1]
    tile = virs // 3
    begin = left // tile
    in_specs = [
        pl.BlockSpec(memory_space=pltpu.SMEM),
        pl.BlockSpec((1, tile), lambda t, place: (0, begin + t)),
        pl.BlockSpec((virs, 1), lambda t, place: (0, 0)),
        pl.BlockSpec((depth, width), lambda t, place: (0, 0)),
        pl.BlockSpec((depth, width), lambda t, place: (0, 0)),
    ]
    operands = []
    for spans, exact, received, offset, lowest in sums:
        shift = begin - lowest // tile
        spec = pl.BlockSpec(
            (1, exact.shape[1], tile),
            functools.partial(lambda offset, shift, t, place: (offset, 0, shift + t), offset, shift),
        )
        in_specs += [spec, spec]
        operands += [exact, received]
    aliases = {}
    if previous is not None:
        in_specs.append(pl.BlockSpec(memory_space=pl.ANY))
        operands.append(previous)
        aliases = {6 + len(operands) - 1: 0}
    in_specs += [pl.BlockSpec(memory_space=pl.ANY)] * len(after)
    operands += after
    return pl.pallas_call(
        functools.partial(gamma_kernel, [spans for spans, *_ in sums], orbital, given, parts),
        grid_spec=pltpu.PrefetchScalarGridSpec(
            num_scalar_prefetch=1,
            grid=((right - left) // tile,),
            in_specs=in_specs,
            out_specs=[
                pl.BlockSpec((1, depth, tile), lambda t, place: (place[OWN] + orbital, 0, begin + t)),
            ] + [pl.BlockSpec((depth // parts, tile), lambda t, place: (0, t))] * parts,
            scratch_shapes=[pltpu.VMEM((width, tile), jnp.bfloat16)],
        ),
        out_shape=[
            jax.ShapeDtypeStruct(whole.shape, whole.dtype),
        ] + [jax.ShapeDtypeStruct((depth // parts, right - left), whole.dtype)] * parts,
        input_output_aliases=aliases,
        compiler_params=params(GAMMA_BYTES),
        cost_estimate=BRIEF,
    )(place, energies, row, column, near, far, *operands)


def turned_kernel(spans, place, energies, row, column, *refs):
    sums, out = refs[:-1], refs[-1]
    for index, (partner, start, stop) in enumerate(spans):
        denominator = (row[...] + column[start:stop]) - energies[place[OWN_ENERGY]] - energies[place[PARTNER_ENERGY + partner]]
        integral = sums[2 * index][0] + sums[2 * index + 1][0].astype(jnp.float32)
        out[:, start:stop] = (integral / denominator).T.astype(jnp.bfloat16)


def turned_amplitudes(place, energies, row, column, sums):
    virs = row.shape[1]
    tile = virs // 3
    in_specs = [
        pl.BlockSpec(memory_space=pltpu.SMEM),
        pl.BlockSpec((1, tile), lambda t, place: (0, t)),
        pl.BlockSpec((virs, 1), lambda t, place: (0, 0)),
    ]
    operands = []
    for _, exact, received, offset, _ in sums:
        spec = pl.BlockSpec((1, exact.shape[1], tile), functools.partial(lambda offset, t, place: (offset, 0, t), offset))
        in_specs += [spec, spec]
        operands += [exact, received]
    return pl.pallas_call(
        functools.partial(turned_kernel, [span for spans, *_ in sums for span in spans]),
        grid_spec=pltpu.PrefetchScalarGridSpec(
            num_scalar_prefetch=1,
            grid=(virs // tile,),
            in_specs=in_specs,
            out_specs=pl.BlockSpec((tile, virs), lambda t, place: (t, 0)),
        ),
        out_shape=jax.ShapeDtypeStruct((virs, virs), jnp.bfloat16),
        compiler_params=params(),
        cost_estimate=BRIEF,
    )(place, energies, row, column, *operands)


def shards(orbital_b, occ_energy, vir_energy):
    occ_index = lax.axis_index("occ")
    aux_index = lax.axis_index("aux")
    occ_count = lax.axis_size("occ")
    aux_count = lax.axis_size("aux")
    chips = aux_count // 2
    rows, depth, virs = orbital_b.shape
    half = rows // 2
    core = aux_index % 2

    def to_mate(value):
        return lax.ppermute(value, "aux", [(at, at ^ 1) for at in range(aux_count)])

    def to_chip(value):
        return lax.ppermute(value, "aux", [(at, (at + 2) % aux_count) for at in range(aux_count)])

    def leader_swap(value):
        pairs = []
        for block in range(occ_count):
            for at in range(aux_count):
                if at % 2:
                    pairs.append((block * aux_count + at, block * aux_count + (at + 2) % aux_count))
                elif block:
                    pairs.append((block * aux_count + at, (block - 1) * aux_count + at))
        return lax.ppermute(value, ("occ", "aux"), pairs)

    place = jnp.stack([
        core * half,
        occ_index * rows + core * half,
        jnp.maximum(occ_index - 1, 0) * rows,
        jnp.minimum(occ_index + 1, occ_count - 1) * rows,
    ]).astype(jnp.int32)

    unit = virs // 3
    spans = [(partner, start, start + unit) for partner in (0, 1) for start in range(0, virs, unit)]
    groups = [(0, half // 2), (half // 2, half - half // 2)]

    near, far = [], []

    def bring(after):
        partner, start, stop = spans[len(near)]
        columns = orbital_b[0, :, start:stop] if after is None else leader_columns(orbital_b, start, stop, after)
        near.append(shifted(columns, "occ", 1 - 2 * partner))
        far.append(to_mate(near[-1]))
        return columns

    bring(None)
    fetched = to_mate(orbital_b)

    steps = [((0,), 0, half - 1, 0, virs), ((0,), half - 1, 1, 0, virs)]
    steps += [((piece,), *group, 0, virs) for piece in (1, 2) for group in groups]
    order = [1, 0, *range(2, half)] if half > 2 else list(range(half))
    steps += [((3, 4, 5), at, 1, 0, virs) for at in order]
    brings = {0: 1, 1: 1, 3: 2, 4: 1}
    ahead = 2 if chips == 2 else 1
    row, column = vir_energy[None, :], vir_energy[:, None]
    arrived, sent, turned, found = [], [], {}, [[] for _ in range(half)]
    rounded = vir_energy
    for at, (pieces, first, count, left, right) in enumerate(steps):
        for piece in pieces:
            if piece not in turned:
                turned[piece] = near[piece].T, far[piece].T
        lead = ahead + (at >= 8) + (at >= 9) if chips == 2 else ahead
        after = [arrived[at - lead] if at >= lead else vir_energy, rounded]
        exact, rounded = partial_integrals(
            place, [turned[piece] for piece in pieces], orbital_b, fetched, first, count, left, right, after
        )
        if len(pieces) > 1 and first == 0 and chips == 2:
            turned_leader = turned_amplitudes(place, occ_energy, row, column, found[0])
            received = leader_swap(jnp.where(core == 0, turned_leader[None], rounded))
        else:
            received = to_chip(rounded) if chips > 1 else jnp.zeros_like(rounded)
        for _ in range(chips - 2):
            exact = exact + received.astype(jnp.float32)
            received = to_chip(received)
        arrived.append(received if chips <= 2 else exact)
        sent.append(rounded)
        for _ in range(brings.get(at, 0)):
            bring(rounded if at else None)
        for offset in range(count):
            found[first + offset].append(([spans[piece] for piece in pieces], exact, received, offset, left))

    leaders = [jnp.concatenate(side, axis=1) for side in (near, far)]
    out, owed = None, []
    for orbital in order:
        while len(owed) > (1 if orbital != order[-1] else 0):
            out = put(out, *owed.pop(0), (1 - core) * half)
        out, *others = gamma_rows(
            place, occ_energy, row, column, *leaders, orbital, 0, virs, found[orbital],
            len(found[orbital]) - 1 if orbital == 0 and chips == 2 else None, orbital_b, out, sent[-1:] if out is None else [],
            1 if orbital == order[-1] or depth % 48 else 3,
        )
        owed.append(([to_mate(other) for other in others], orbital, 0))
    while owed:
        out = put(out, *owed.pop(0), (1 - core) * half)
    return out


def put(out, parts, orbital, left, offset):
    zero = jnp.zeros((), jnp.int32)
    for part, value in enumerate(parts):
        out = lax.dynamic_update_slice(out, value[None], (offset + orbital, zero + part * value.shape[0], zero + left))
    return out


def solution(mesh):
    placed = (P("occ", "aux", None), P(), P())
    return jax.shard_map(
        shards, mesh=mesh, in_specs=placed, out_specs=P("occ", "aux", None), check_vma=False
    )
```

```python
import functools

import jax
import jax.numpy as jnp
from jax import lax
from jax.experimental import pallas as pl
from jax.experimental.pallas import tpu as pltpu
from jax.sharding import PartitionSpec as P

VMEM_BYTES = 56 * 1024 * 1024
GAMMA_BYTES = 40 * 1024 * 1024

BRIEF = pl.CostEstimate(flops=0, bytes_accessed=0, transcendentals=0)

OWN, OWN_ENERGY, PARTNER_ENERGY = 0, 1, 2


def shifted(value, axis, steps):
    count = lax.axis_size(axis)
    initial, last = (max(0, -steps), min(count, count - steps))
    return lax.ppermute(value, axis, [(source, source + steps) for source in range(initial, last)])


def params(limit=VMEM_BYTES):
    return pltpu.CompilerParams(vmem_limit_bytes=limit)


def columns_kernel(source, after, out):
    out[...] = source[0]


def leader_columns(orbital_b, start, stop, after):
    depth = orbital_b.shape[1]
    width = 128 if (start % 128 == 0 and stop % 128 == 0) else stop - start
    return pl.pallas_call(
        columns_kernel,
        grid=((stop - start) // width,),
        in_specs=[
            pl.BlockSpec((1, depth, width), lambda t: (0, 0, start // width + t)),
            pl.BlockSpec(memory_space=pl.ANY),
        ],
        out_specs=pl.BlockSpec((depth, width), lambda t: (0, t)),
        out_shape=jax.ShapeDtypeStruct((depth, stop - start), orbital_b.dtype),
        compiler_params=params(),
        cost_estimate=BRIEF,
    )(orbital_b, after)


def partial_kernel(pieces, place, *refs):
    near_b, far_b = refs[2 * pieces : 2 * pieces + 2]
    exact, rounded = refs[-2:]
    at = 0
    for piece in range(pieces):
        near, far = refs[2 * piece : 2 * piece + 2]
        total = jnp.dot(near[...], near_b[0], preferred_element_type=jnp.float32)
        total += jnp.dot(far[...], far_b[0], preferred_element_type=jnp.float32)
        here = slice(at, at + near.shape[0])
        exact[0, here] = total
        rounded[0, here] = total.astype(jnp.bfloat16)
        at += near.shape[0]


def partial_integrals(place, leaders, orbital_b, fetched, first, count, left, right, after):
    depth, virs = orbital_b.shape[1:]
    width = sum(near.shape[0] for near, _ in leaders)
    tile = right - left if (right - left) == virs or left % 128 else virs // 3
    begin = left // tile
    own = pl.BlockSpec((1, depth, tile), lambda i, t, place: (place[OWN] + first + i, 0, begin + t))
    grid_spec = pltpu.PrefetchScalarGridSpec(
        num_scalar_prefetch=1,
        grid=(count, (right - left) // tile),
        in_specs=[pl.BlockSpec(side.shape, lambda i, t, place: (0, 0)) for pair in leaders for side in pair]
        + [own, own] + [pl.BlockSpec(memory_space=pl.ANY)] * len(after),
        out_specs=[pl.BlockSpec((1, width, tile), lambda i, t, place: (i, 0, t))] * 2,
    )
    return pl.pallas_call(
        functools.partial(partial_kernel, len(leaders)),
        grid_spec=grid_spec,
        out_shape=[
            jax.ShapeDtypeStruct((count, width, right - left), jnp.float32),
            jax.ShapeDtypeStruct((count, width, right - left), jnp.bfloat16),
        ],
        compiler_params=params(),
        cost_estimate=BRIEF,
    )(place, *[side for pair in leaders for side in pair], orbital_b, fetched, *after)


def gamma_kernel(spans, orbital, given, parts, place, energies, row, column, near, far, *refs):
    own, outs, amplitude = refs[-2 - parts], refs[-1 - parts : -1], refs[-1]
    own_energy = energies[place[OWN_ENERGY] + orbital]
    at = 0
    for index, ranges in enumerate(spans):
        exact, received = refs[2 * index], refs[2 * index + 1]
        lowest = 0
        for partner, start, stop in ranges:
            here = slice(lowest, lowest + stop - start)
            denominator = (row[...] + column[start:stop]) - own_energy - energies[place[PARTNER_ENERGY + partner]]
            other = received[0, here].astype(jnp.float32)
            value = (exact[0, here] + other) / denominator
            if index == given:
                value = jnp.where(place[OWN] == 0, other, value)
            amplitude[at : at + stop - start] = value.astype(jnp.bfloat16)
            lowest += stop - start
            at += stop - start
    own[0] = jnp.dot(near[...], amplitude[...], preferred_element_type=jnp.float32).astype(own.dtype)
    other = jnp.dot(far[...], amplitude[...], preferred_element_type=jnp.float32).astype(own.dtype)
    rows = other.shape[0] // parts
    for part, out in enumerate(outs):
        out[...] = other[part * rows : (part + 1) * rows]


def gamma_rows(place, energies, row, column, near, far, orbital, left, right, sums, given, whole, previous, after, parts):
    depth, width = near.shape
    virs = row.shape[1]
    tile = virs // 3
    begin = left // tile
    in_specs = [
        pl.BlockSpec(memory_space=pltpu.SMEM),
        pl.BlockSpec((1, tile), lambda t, place: (0, begin + t)),
        pl.BlockSpec((virs, 1), lambda t, place: (0, 0)),
        pl.BlockSpec((depth, width), lambda t, place: (0, 0)),
        pl.BlockSpec((depth, width), lambda t, place: (0, 0)),
    ]
    operands = []
    for spans, exact, received, offset, lowest in sums:
        shift = begin - lowest // tile
        spec = pl.BlockSpec(
            (1, exact.shape[1], tile),
            functools.partial(lambda offset, shift, t, place: (offset, 0, shift + t), offset, shift),
        )
        in_specs += [spec, spec]
        operands += [exact, received]
    aliases = {}
    if previous is not None:
        in_specs.append(pl.BlockSpec(memory_space=pl.ANY))
        operands.append(previous)
        aliases = {6 + len(operands) - 1: 0}
    in_specs += [pl.BlockSpec(memory_space=pl.ANY)] * len(after)
    operands += after
    return pl.pallas_call(
        functools.partial(gamma_kernel, [spans for spans, *_ in sums], orbital, given, parts),
        grid_spec=pltpu.PrefetchScalarGridSpec(
            num_scalar_prefetch=1,
            grid=((right - left) // tile,),
            in_specs=in_specs,
            out_specs=[
                pl.BlockSpec((1, depth, tile), lambda t, place: (place[OWN] + orbital, 0, begin + t)),
            ] + [pl.BlockSpec((depth // parts, tile), lambda t, place: (0, t))] * parts,
            scratch_shapes=[pltpu.VMEM((width, tile), jnp.bfloat16)],
        ),
        out_shape=[
            jax.ShapeDtypeStruct(whole.shape, whole.dtype),
        ] + [jax.ShapeDtypeStruct((depth // parts, right - left), whole.dtype)] * parts,
        input_output_aliases=aliases,
        compiler_params=params(GAMMA_BYTES),
        cost_estimate=BRIEF,
    )(place, energies, row, column, near, far, *operands)


def turned_kernel(spans, place, energies, row, column, *refs):
    sums, out = refs[:-1], refs[-1]
    for index, (partner, start, stop) in enumerate(spans):
        denominator = (row[...] + column[start:stop]) - energies[place[OWN_ENERGY]] - energies[place[PARTNER_ENERGY + partner]]
        integral = sums[2 * index][0] + sums[2 * index + 1][0].astype(jnp.float32)
        out[:, start:stop] = (integral / denominator).T.astype(jnp.bfloat16)


def turned_amplitudes(place, energies, row, column, sums):
    virs = row.shape[1]
    tile = virs // 3
    in_specs = [
        pl.BlockSpec(memory_space=pltpu.SMEM),
        pl.BlockSpec((1, tile), lambda t, place: (0, t)),
        pl.BlockSpec((virs, 1), lambda t, place: (0, 0)),
    ]
    operands = []
    for _, exact, received, offset, _ in sums:
        spec = pl.BlockSpec((1, exact.shape[1], tile), functools.partial(lambda offset, t, place: (offset, 0, t), offset))
        in_specs += [spec, spec]
        operands += [exact, received]
    return pl.pallas_call(
        functools.partial(turned_kernel, [span for spans, *_ in sums for span in spans]),
        grid_spec=pltpu.PrefetchScalarGridSpec(
            num_scalar_prefetch=1,
            grid=(virs // tile,),
            in_specs=in_specs,
            out_specs=pl.BlockSpec((tile, virs), lambda t, place: (t, 0)),
        ),
        out_shape=jax.ShapeDtypeStruct((virs, virs), jnp.bfloat16),
        compiler_params=params(),
        cost_estimate=BRIEF,
    )(place, energies, row, column, *operands)


def shards(orbital_b, occ_energy, vir_energy):
    occ_index = lax.axis_index("occ")
    aux_index = lax.axis_index("aux")
    occ_count = lax.axis_size("occ")
    aux_count = lax.axis_size("aux")
    chips = aux_count // 2
    rows, depth, virs = orbital_b.shape
    half = rows // 2
    core = aux_index % 2

    def to_mate(value):
        return lax.ppermute(value, "aux", [(at, at ^ 1) for at in range(aux_count)])

    def to_chip(value):
        return lax.ppermute(value, "aux", [(at, (at + 2) % aux_count) for at in range(aux_count)])

    def leader_swap(value):
        pairs = []
        for block in range(occ_count):
            for at in range(aux_count):
                if at % 2:
                    pairs.append((block * aux_count + at, block * aux_count + (at + 2) % aux_count))
                elif block:
                    pairs.append((block * aux_count + at, (block - 1) * aux_count + at))
        return lax.ppermute(value, ("occ", "aux"), pairs)

    place = jnp.stack([
        core * half,
        occ_index * rows + core * half,
        jnp.maximum(occ_index - 1, 0) * rows,
        jnp.minimum(occ_index + 1, occ_count - 1) * rows,
    ]).astype(jnp.int32)

    unit = virs // 3
    spans = [(partner, start, start + unit) for partner in (0, 1) for start in range(0, virs, unit)]
    groups = [(0, half // 2), (half // 2, half - half // 2)]

    near, far = [], []

    def bring(after):
        partner, start, stop = spans[len(near)]
        columns = orbital_b[0, :, start:stop] if after is None else leader_columns(orbital_b, start, stop, after)
        near.append(shifted(columns, "occ", 1 - 2 * partner))
        far.append(to_mate(near[-1]))
        return columns

    bring(None)
    fetched = to_mate(orbital_b)

    steps = [((0,), 0, half - 1, 0, virs), ((0,), half - 1, 1, 0, virs)]
    steps += [((piece,), *group, 0, virs) for piece in (1, 2) for group in groups]
    order = [1, 0, *range(2, half)] if half > 2 else list(range(half))
    steps += [((3, 4, 5), at, 1, 0, virs) for at in order]
    brings = {0: 1, 1: 1, 3: 2, 4: 1}
    ahead = 2 if chips == 2 else 1
    row, column = vir_energy[None, :], vir_energy[:, None]
    arrived, sent, turned, found = [], [], {}, [[] for _ in range(half)]
    rounded = vir_energy
    for at, (pieces, first, count, left, right) in enumerate(steps):
        for piece in pieces:
            if piece not in turned:
                turned[piece] = near[piece].T, far[piece].T
        lead = ahead + (at >= 8) + (at >= 9) if chips == 2 else ahead
        after = [arrived[at - lead] if at >= lead else vir_energy, rounded]
        if chips == 2 and at in (2, 3):
            after = [rounded] if at == 2 else [*arrived[:2], rounded]
        exact, rounded = partial_integrals(
            place, [turned[piece] for piece in pieces], orbital_b, fetched, first, count, left, right, after
        )
        if len(pieces) > 1 and first == 0 and chips == 2:
            turned_leader = turned_amplitudes(place, occ_energy, row, column, found[0])
            received = leader_swap(jnp.where(core == 0, turned_leader[None], rounded))
        else:
            received = to_chip(rounded) if chips > 1 else jnp.zeros_like(rounded)
        for _ in range(chips - 2):
            exact = exact + received.astype(jnp.float32)
            received = to_chip(received)
        arrived.append(received if chips <= 2 else exact)
        sent.append(rounded)
        for _ in range(brings.get(at, 0)):
            bring(rounded if at else None)
        for offset in range(count):
            found[first + offset].append(([spans[piece] for piece in pieces], exact, received, offset, left))

    leaders = [jnp.concatenate(side, axis=1) for side in (near, far)]
    out, owed = None, []
    for orbital in order:
        while len(owed) > (1 if orbital != order[-1] else 0):
            out = put(out, *owed.pop(0), (1 - core) * half)
        out, *others = gamma_rows(
            place, occ_energy, row, column, *leaders, orbital, 0, virs, found[orbital],
            len(found[orbital]) - 1 if orbital == 0 and chips == 2 else None, orbital_b, out, sent[-1:] if out is None else [],
            1 if orbital == order[-1] or depth % 48 else 3,
        )
        owed.append(([to_mate(other) for other in others], orbital, 0))
    while owed:
        out = put(out, *owed.pop(0), (1 - core) * half)
    return out


def put(out, parts, orbital, left, offset):
    zero = jnp.zeros((), jnp.int32)
    for part, value in enumerate(parts):
        out = lax.dynamic_update_slice(out, value[None], (offset + orbital, zero + part * value.shape[0], zero + left))
    return out


def solution(mesh):
    placed = (P("occ", "aux", None), P(), P())
    return jax.shard_map(
        shards, mesh=mesh, in_specs=placed, out_specs=P("occ", "aux", None), check_vma=False
    )
```
